256 devices in a mesh: dp: 8 (over y, z_hi), token: 32 (over x, z_lo, core).
Axes of the slice: x: 4, y: 4, z: 8 (z_hi: 2, z_lo: 4; z = z_hi * 4 + z_lo), core: 2. Of those that a mesh axis runs over, the one named last changes fastest.
Arguments:
- tokens: bfloat16 [2048, 32, 1024], P('dp', 'token'), may hold values from -6 to 6
- w_up: bfloat16 [32, 1024, 4096], P('token', None, 'dp'), may hold values from -0.1875 to 0.1875
- w_down: bfloat16 [32, 4096, 1024], P('token', 'dp'), may hold values from -0.09375 to 0.09375
- cotangent: bfloat16 [2048, 32, 1024], P('dp', 'token'), may hold values from -6 to 6
Outputs:
- output: bfloat16 [2048, 32, 1024], P('dp', 'token')
- grad_tokens: bfloat16 [2048, 32, 1024], P('dp', 'token')
- grad_up: float32 [32, 1024, 4096], P('token', None, 'dp')
- grad_down: float32 [32, 4096, 1024], P('token', 'dp')
The draws below stay inside these ranges and needn't reach their ends.
All inputs are finite; a program needn't handle non-finite values.
Results may differ from the reference program's by a relative error of at most 0.014.
Values may be sent and summed in bfloat16 or wider, within the bound.
A program may use at most 128 MiB of HBM per device.

```python
import jax
import jax.numpy as jnp
from jax import lax

D = 1024
FF = 4096
TOKENS = 32
SAMPLES = 2048
N_DP = 8


def steps_of(stream_key, dims, shards, low, largest):
    def one(axis_at, blocks):
        draws = jax.random.uniform(jax.random.fold_in(jax.random.fold_in(stream_key, 6), axis_at), (blocks,), jnp.float32, low / len(shards), largest / len(shards))
        return jnp.repeat(jnp.exp(draws), dims[axis_at] // blocks).reshape((-1,) + (1,) * (len(dims) - axis_at - 1))

    gain = one(*shards[0])
    for cut in shards[1:]:
        gain = gain * one(*cut)
    return gain


def noise(rng, shape, deviation, limit, split=(), dtype=jnp.bfloat16):
    values = deviation * jax.random.normal(rng, shape, jnp.float32)
    if split:
        values = values * steps_of(rng, shape, split, -0.22, 0.18)
    return jnp.clip(values, -limit, limit).astype(dtype)


def setup_inputs(seed: int = 0) -> dict:
    streams_of = jax.random.split(jax.random.key(seed), 5)
    tokens = noise(streams_of[0], (SAMPLES, TOKENS, D), 1.0, 6.0, ((0, 8), (1, 32)))
    w_up = noise(streams_of[1], (TOKENS, D, FF), D ** -0.5, 0.1875, ((0, 32), (2, 8)))
    w_down = noise(streams_of[2], (TOKENS, FF, D), FF ** -0.5, 0.09375, ((0, 32), (1, 8)))
    cotangent = noise(streams_of[3], (SAMPLES, TOKENS, D), 1.0, 6.0, ((0, 8), (1, 32)))
    return dict(tokens=tokens, w_up=w_up, w_down=w_down, cotangent=cotangent)


EPSILON = 1e-05

def layer_norm(values):
    average = lax.optimization_barrier(jnp.mean(values, axis=-1, keepdims=True))
    centred = values - average
    spread = lax.optimization_barrier(jnp.mean(centred * centred, axis=-1, keepdims=True))
    scaling = lax.rsqrt(spread + EPSILON)
    return (centred * scaling, scaling)

def norm_back(normed, scaling, upstream):
    first = lax.optimization_barrier(jnp.mean(upstream, axis=-1, keepdims=True))
    second = lax.optimization_barrier(jnp.mean(upstream * normed, axis=-1, keepdims=True))
    return scaling * (upstream - first - normed * second)

def gelu_slope(hidden):
    return jax.grad(lambda inner: jnp.sum(jax.nn.gelu(inner)))(hidden)

def token_mix(blocks):
    sample_count, token_count, feature_width = blocks.shape
    split_heads = blocks.reshape(sample_count, token_count, token_count, feature_width // token_count)
    return split_heads.transpose(0, 2, 1, 3).reshape(sample_count, token_count, feature_width)

def reference(tokens, w_up, w_down, cotangent):
    sample_count = tokens.shape[0]
    slice_width = FF // N_DP
    mixed_in = token_mix(tokens)
    summed = mixed_in.astype(jnp.float32) + tokens.astype(jnp.float32)
    normed_in, scale_in = layer_norm(summed)
    shared = normed_in.astype(jnp.bfloat16)

    def per_token(operands):
        shared_tok, up_mat, down_mat, cotan_tok = operands
        hidden = jnp.dot(shared_tok, up_mat, preferred_element_type=jnp.float32)
        activ = jax.nn.gelu(hidden).astype(jnp.bfloat16)
        act_groups = activ.astype(jnp.float32).reshape(sample_count, N_DP, slice_width)
        down_groups = down_mat.astype(jnp.float32).reshape(N_DP, slice_width, D)
        partials = jnp.einsum('sgf,gfd->gsd', act_groups, down_groups)
        rounded = lax.optimization_barrier(partials.astype(jnp.bfloat16))
        ffn = lax.optimization_barrier(jnp.sum(rounded.astype(jnp.float32), axis=0))
        normed_out, scale_out = layer_norm(ffn + shared_tok.astype(jnp.float32))
        out_tok = normed_out.astype(jnp.bfloat16)
        grad_out = norm_back(normed_out, scale_out, cotan_tok.astype(jnp.float32))
        grad_ffn = grad_out.astype(jnp.bfloat16)
        grad_down = jnp.dot(activ.T, grad_ffn, preferred_element_type=jnp.float32)
        grad_act = jnp.dot(grad_ffn, down_mat.T, preferred_element_type=jnp.float32)
        grad_hidden = (grad_act * gelu_slope(hidden)).astype(jnp.bfloat16)
        grad_up = jnp.dot(shared_tok.T, grad_hidden, preferred_element_type=jnp.float32)
        hid_groups = grad_hidden.astype(jnp.float32).reshape(sample_count, N_DP, slice_width)
        up_groups = up_mat.astype(jnp.float32).reshape(D, N_DP, slice_width)
        back_parts = jnp.einsum('sgf,dgf->gsd', hid_groups, up_groups)
        back_round = lax.optimization_barrier(back_parts.astype(jnp.bfloat16))
        grad_shared = grad_out + lax.optimization_barrier(jnp.sum(back_round.astype(jnp.float32), axis=0))
        return (out_tok, grad_shared, grad_up, grad_down)
    shared_t = shared.transpose(1, 0, 2)
    cotan_t = cotangent.transpose(1, 0, 2)
    out_all, grad_shared, grad_up, grad_down = lax.map(per_token, (shared_t, w_up, w_down, cotan_t))
    output = out_all.transpose(1, 0, 2)
    grad_shared = grad_shared.transpose(1, 0, 2)
    grad_summed = norm_back(normed_in, scale_in, grad_shared)
    back_mixed = token_mix(grad_summed.astype(jnp.bfloat16))
    grad_tokens = (grad_summed + back_mixed.astype(jnp.float32)).astype(jnp.bfloat16)
    return (output, grad_tokens, grad_up, grad_down)
```

```python
import jax
import jax.numpy as jnp
from jax import lax
from jax.sharding import PartitionSpec as P

TOKENS = 32


EPSILON = 1e-05


def layer_norm(values):
    average = jnp.mean(values, axis=-1, keepdims=True)
    centred = values - average
    spread = jnp.mean(centred * centred, axis=-1, keepdims=True)
    scaling = lax.rsqrt(spread + EPSILON)
    return (centred * scaling, scaling)


def norm_back(normed, scaling, upstream):
    first = jnp.mean(upstream, axis=-1, keepdims=True)
    second = jnp.mean(upstream * normed, axis=-1, keepdims=True)
    return scaling * (upstream - first - normed * second)


def gelu_slope(hidden):
    return jax.grad(lambda inner: jnp.sum(jax.nn.gelu(inner)))(hidden)


def on_device(tokens, w_up, w_down, cotangent):
    local_rows, owned, feature_width = tokens.shape
    head_size = feature_width // TOKENS
    split_heads = tokens.reshape(local_rows, owned, TOKENS, head_size)
    arrived = lax.all_to_all(split_heads, "token", split_axis=2, concat_axis=1, tiled=True)
    mixed_in = arrived.transpose(0, 2, 1, 3).reshape(local_rows, owned, feature_width)
    summed = mixed_in.astype(jnp.float32) + tokens.astype(jnp.float32)
    normed_in, scale_in = layer_norm(summed)
    shared = normed_in.astype(jnp.bfloat16)
    all_shared = lax.all_gather(shared, "dp", axis=0, tiled=True)
    hidden = jnp.einsum("spd,pdf->spf", all_shared, w_up, preferred_element_type=jnp.float32)
    activ = jax.nn.gelu(hidden).astype(jnp.bfloat16)
    term_all = jnp.einsum("spf,pfd->spd", activ, w_down, preferred_element_type=jnp.float32)
    ffn = lax.psum_scatter(
        term_all.astype(jnp.bfloat16), "dp", scatter_dimension=0, tiled=True
    ).astype(jnp.float32)
    normed_out, scale_out = layer_norm(ffn + shared.astype(jnp.float32))
    output = normed_out.astype(jnp.bfloat16)
    grad_out = norm_back(normed_out, scale_out, cotangent.astype(jnp.float32))
    grad_ffn = lax.all_gather(grad_out.astype(jnp.bfloat16), "dp", axis=0, tiled=True)
    grad_down = jnp.einsum("spf,spd->pfd", activ, grad_ffn, preferred_element_type=jnp.float32)
    grad_act = jnp.einsum("spd,pfd->spf", grad_ffn, w_down, preferred_element_type=jnp.float32)
    grad_hidden = (grad_act * gelu_slope(hidden)).astype(jnp.bfloat16)
    grad_up = jnp.einsum(
        "spd,spf->pdf", all_shared, grad_hidden, preferred_element_type=jnp.float32
    )
    grad_back = lax.psum_scatter(
        jnp.einsum("spf,pdf->spd", grad_hidden, w_up, preferred_element_type=jnp.float32).astype(
            jnp.bfloat16
        ),
        "dp",
        scatter_dimension=0,
        tiled=True,
    ).astype(jnp.float32)
    grad_shared = grad_back + grad_out
    grad_summed = norm_back(normed_in, scale_in, grad_shared)
    back_heads = grad_summed.astype(jnp.bfloat16).reshape(local_rows, owned, TOKENS, head_size)
    returned = lax.all_to_all(back_heads, "token", split_axis=2, concat_axis=1, tiled=True)
    back_mixed = returned.transpose(0, 2, 1, 3).reshape(local_rows, owned, feature_width)
    grad_tokens = (grad_summed + back_mixed.astype(jnp.float32)).astype(jnp.bfloat16)
    return (output, grad_tokens, grad_up, grad_down)


def solution(mesh):
    in_specs = (
        P("dp", "token", None),
        P("token", None, "dp"),
        P("token", "dp", None),
        P("dp", "token", None),
    )
    out_specs = (
        P("dp", "token", None),
        P("dp", "token", None),
        P("token", None, "dp"),
        P("token", "dp", None),
    )
    return jax.shard_map(
        on_device, mesh=mesh, in_specs=in_specs, out_specs=out_specs, check_vma=False
    )
```

```python
import functools

import jax
import jax.numpy as jnp
from jax import lax
from jax.experimental import pallas as pl
from jax.experimental.pallas import tpu as pltpu
from jax.sharding import PartitionSpec as P

MESH = pl.DeviceIdType.MESH
EPSILON = 1e-05
CHUNKS = 2
LANES = 128
GROUP = 4
WIDE = GROUP * LANES
MXU_ROWS = 256
F32 = jnp.float32
BF16 = jnp.bfloat16

MIX, MIX_BACK, UP, DOWN, GRAD_UP, GRAD_DOWN = 0, 2, 4, 5, 6, 7
GATHER, SCATTER, GATHER_BACK, SCATTER_BACK = 8, 14, 18, 24
COPIES = 28


def dot_nn(a, b):
    return jnp.dot(a, b, preferred_element_type=F32)


def dot_nt(a, b):
    return lax.dot_general(a, b, (((1,), (1,)), ((), ())), preferred_element_type=F32)


def layer_norm(values):
    centred = values - jnp.mean(values, axis=0, keepdims=True)
    scaling = lax.rsqrt(jnp.mean(centred * centred, axis=0, keepdims=True) + EPSILON)
    return centred * scaling, scaling


def norm_back(normed, scaling, upstream):
    first = jnp.mean(upstream, axis=0, keepdims=True)
    second = jnp.mean(upstream * normed, axis=0, keepdims=True)
    return scaling * (upstream - first - normed * second)


def gelu_and_slope(v):
    root = 0.7978845608028654
    square = v * v
    t = jnp.tanh(v * (root + (root * 0.044715) * square))
    half = 0.5 * (1.0 + t)
    inner = root + (3.0 * root * 0.044715) * square
    slope = half + (0.5 * v) * (1.0 - t * t) * inner
    return v * half, slope


def kernel(
    n_token, head,
    tok_ref, up_ref, down_ref, cot_ref,
    out_ref, gtok_ref, gup_ref, gdown_ref,
    tok_t, mixed, cot_t, up_far, down_far, up_t, down_t,
    shared, activ, slope, gffn, ghid,
    part_f, near_f, pass_f, far_f, part_b, near_b, pass_b, far_b,
    normed, scale_in, gout, gsum, gsum16, mixed_back,
    gup_out, gup_in, gdown_out, gdown_in,
    send, recv,
):
    dp = lax.axis_index("dp")
    me = lax.axis_index("token")
    y, zh = dp // 2, dp % 2
    dev_y = ((y + 1 - 2 * (y % 2)) * 2 + zh, me)
    dev_z = (y * 2 + 1 - zh, me)
    dev_w = ((3 - y) * 2 + zh, me)
    d_model, own = up_ref.shape

    def remote(src, dst, sem, device):
        return pltpu.make_async_remote_copy(
            src_ref=src, dst_ref=dst, send_sem=send.at[sem], recv_sem=recv.at[sem],
            device_id=device, device_id_type=MESH,
        )

    def piece(ref, c, p, n=1):
        return ref.at[:, pl.ds(c * WIDE + p * LANES, n * LANES)]

    def rows(i, n):
        return pl.ds(pl.multiple_of(i * n, n), n)

    barrier = pltpu.get_barrier_semaphore()

    @pl.loop(1, n_token)
    def _(i):
        pl.semaphore_signal(barrier, inc=1, device_id=(dp, (me + i) % n_token), device_id_type=MESH)

    for device in (dev_y, dev_z, dev_w):
        pl.semaphore_signal(barrier, inc=1, device_id=device, device_id_type=MESH)

    @pl.loop(0, d_model // LANES)
    def _(i):
        block = tok_ref[:, rows(i, LANES)].T
        for c in range(CHUNKS):
            tok_t[c, rows(i, LANES), :] = block[:, c * LANES:(c + 1) * LANES]

    pl.semaphore_wait(barrier, n_token + 2)

    w_up = remote(up_ref, up_far, UP, dev_w)
    w_down = remote(down_ref, down_far, DOWN, dev_w)

    def mix_start(src, dst, sem, c):
        @pl.loop(1, n_token)
        def _(i):
            to = (me + i) % n_token
            remote(
                src.at[c, rows(to, head), :], dst.at[c, rows(me, head), :], sem + c, (dp, to)
            ).start()

        dst[c, rows(me, head), :] = src[c, rows(me, head), :]

    def mix_wait(src, dst, sem, c):
        span = pl.ds(0, (n_token - 1) * head)
        whole = remote(src.at[c, span, :], dst.at[c, span, :], sem + c, dev_y)
        whole.wait_send()
        whole.wait_recv()

    def gather(ref, sem, c):
        return (
            remote(piece(ref, c, 0), piece(ref, c, 2), sem + c, dev_y),
            remote(piece(ref, c, 0), piece(ref, c, 1), sem + 2 + c, dev_z),
            remote(piece(ref, c, 1), piece(ref, c, 3), sem + 4 + c, dev_y),
        )

    def scatter(part, near, passed, far, sem, c):
        return (
            remote(piece(part, c, 2, 2), near.at[c], sem + c, dev_y),
            remote(passed.at[c], far.at[c], sem + 2 + c, dev_z),
        )

    gathers = [gather(shared, GATHER, c) for c in range(CHUNKS)]
    scatters = [scatter(part_f, near_f, pass_f, far_f, SCATTER, c) for c in range(CHUNKS)]
    gathers_b = [gather(gffn, GATHER_BACK, c) for c in range(CHUNKS)]
    scatters_b = [scatter(part_b, near_b, pass_b, far_b, SCATTER_BACK, c) for c in range(CHUNKS)]
    g_up = remote(gup_out, gup_in, GRAD_UP, dev_w)
    g_down = remote(gdown_out, gdown_in, GRAD_DOWN, dev_w)

    def transpose_up(src, half):
        @pl.loop(0, own // LANES)
        def _(i):
            up_t[pl.ds(pl.multiple_of(half * own + i * LANES, LANES), LANES), :] = src[:, rows(i, LANES)].T

    def transpose_down(src, half):
        @pl.loop(0, d_model // LANES)
        def _(i):
            down_t[rows(i, LANES), pl.ds(half * own, own)] = src[:, rows(i, LANES)].T

    def norm_in(c):
        summed = mixed[c].astype(F32) + tok_t[c].astype(F32)
        value, scaling = layer_norm(summed)
        normed[c] = value
        scale_in[c, 0:1, :] = scaling
        shared[:, c * WIDE:c * WIDE + LANES] = value.astype(BF16)

    def up(c):
        span = pl.ds(c * WIDE, WIDE)

        @pl.loop(0, 2 * own // MXU_ROWS)
        def _(i):
            r = rows(i, MXU_ROWS)
            hidden = dot_nn(up_t[r, :], shared[:, span])
            value, grade = gelu_and_slope(hidden)
            activ[r, span] = value.astype(BF16)
            slope[r, span] = grade.astype(BF16)

    def down(c, p):
        span = pl.ds(c * WIDE + p * LANES, 2 * LANES)

        @pl.loop(0, d_model // MXU_ROWS)
        def _(i):
            r = rows(i, MXU_ROWS)
            part_f[r, span] = dot_nn(down_t[r, :], activ[:, span]).astype(BF16)

    def add_near(part, near, passed, c):
        passed[c] = (
            part[:, c * WIDE + LANES:c * WIDE + 2 * LANES].astype(F32) + near[c, :, LANES:].astype(F32)
        ).astype(BF16)

    def total(part, near, far, c):
        return (
            part[:, c * WIDE:c * WIDE + LANES].astype(F32)
            + near[c, :, :LANES].astype(F32)
            + far[c].astype(F32)
        )

    def norm_out(c):
        ffn = total(part_f, near_f, far_f, c)
        value, scaling = layer_norm(ffn + shared[:, c * WIDE:c * WIDE + LANES].astype(F32))
        part_f[:, c * WIDE:c * WIDE + LANES] = value.astype(BF16)
        grad = norm_back(value, scaling, cot_t[c].astype(F32))
        gout[c] = grad
        gffn[:, c * WIDE:c * WIDE + LANES] = grad.astype(BF16)

    def write_out(c):
        @pl.loop(0, d_model // LANES)
        def _(i):
            out_ref[pl.ds(c * LANES, LANES), rows(i, LANES)] = part_f[rows(i, LANES), pl.ds(c * WIDE, LANES)].T

    def hidden_back(c):
        span = pl.ds(c * WIDE, WIDE)
        for half, src in enumerate((down_ref, down_far)):
            @pl.loop(0, own // MXU_ROWS)
            def _(i):
                r = pl.ds(pl.multiple_of(half * own + i * MXU_ROWS, MXU_ROWS), MXU_ROWS)
                grad = dot_nn(src[rows(i, MXU_ROWS), :], gffn[:, span])
                ghid[r, span] = (grad * slope[r, span].astype(F32)).astype(BF16)

    def shared_back(c, p):
        span = pl.ds(c * WIDE + p * LANES, 2 * LANES)

        @pl.loop(0, d_model // MXU_ROWS)
        def _(i):
            r = rows(i, MXU_ROWS)
            part_b[r, span] = (
                dot_nn(up_ref[r, :], ghid[pl.ds(0, own), span])
                + dot_nn(up_far[r, :], ghid[pl.ds(own, own), span])
            ).astype(BF16)

    def sum_back(c):
        grad = total(part_b, near_b, far_b, c) + gout[c]
        grad = norm_back(normed[c], scale_in[c, 0:1, :], grad)
        gsum[c] = grad
        gsum16[c] = grad.astype(BF16)

    def tokens_back(c):
        @pl.loop(0, d_model // LANES)
        def _(i):
            r = rows(i, LANES)
            value = (gsum[c, r, :] + mixed_back[c, r, :].astype(F32)).astype(BF16)
            gtok_ref[pl.ds(c * LANES, LANES), r] = value.T

    def grad_down(half, dst):
        @pl.loop(0, own // MXU_ROWS)
        def _(i):
            r = pl.ds(pl.multiple_of(half * own + i * MXU_ROWS, MXU_ROWS), MXU_ROWS)
            dst[rows(i, MXU_ROWS), :] = dot_nt(activ[r, :], gffn[...]).astype(dst.dtype)

    def grad_up(half, dst):
        @pl.loop(0, d_model // MXU_ROWS)
        def _(i):
            r = rows(i, MXU_ROWS)
            dst[r, :] = dot_nt(shared[r, :], ghid[pl.ds(half * own, own), :]).astype(dst.dtype)

    for c in range(CHUNKS):
        mix_start(tok_t, mixed, MIX, c)
    w_up.start()
    w_down.start()
    transpose_up(up_ref, 0)
    transpose_down(down_ref, 0)

    @pl.loop(0, d_model // LANES)
    def _(i):
        block = cot_ref[:, rows(i, LANES)].T
        for c in range(CHUNKS):
            cot_t[c, rows(i, LANES), :] = block[:, c * LANES:(c + 1) * LANES]

    for c in range(CHUNKS):
        mix_wait(tok_t, mixed, MIX, c)
        norm_in(c)
        gathers[c][0].start()
        gathers[c][1].start()
    w_up.wait_recv()
    transpose_up(up_far, 1)
    for c in range(CHUNKS):
        gathers[c][1].wait_recv()
        gathers[c][2].start()
    for c in range(CHUNKS):
        gathers[c][0].wait_recv()
        gathers[c][2].wait_recv()
        up(c)
    w_down.wait_recv()
    transpose_down(down_far, 1)
    for c in range(CHUNKS):
        down(c, 2)
        scatters[c][0].start()
        down(c, 0)
    for c in range(CHUNKS):
        scatters[c][0].wait_recv()
        add_near(part_f, near_f, pass_f, c)
        scatters[c][1].start()
    for c in range(CHUNKS):
        scatters[c][1].wait_recv()
        norm_out(c)
        gathers_b[c][0].start()
        gathers_b[c][1].start()
    for c in range(CHUNKS):
        write_out(c)
    for c in range(CHUNKS):
        gathers_b[c][1].wait_recv()
        gathers_b[c][2].start()
    for c in range(CHUNKS):
        gathers_b[c][0].wait_recv()
        gathers_b[c][2].wait_recv()
        if c == CHUNKS - 1:
            grad_down(1, gdown_out)
            g_down.start()
        hidden_back(c)
        shared_back(c, 2)
        scatters_b[c][0].start()
        shared_back(c, 0)
    grad_up(1, gup_out)
    g_up.start()
    for c in range(CHUNKS):
        scatters_b[c][0].wait_recv()
        add_near(part_b, near_b, pass_b, c)
        scatters_b[c][1].start()
    grad_down(0, gdown_ref)
    for c in range(CHUNKS):
        scatters_b[c][1].wait_recv()
        sum_back(c)
        mix_start(gsum16, mixed_back, MIX_BACK, c)
    grad_up(0, gup_ref)
    for c in range(CHUNKS):
        mix_wait(gsum16, mixed_back, MIX_BACK, c)
        tokens_back(c)
    g_down.wait_recv()
    gdown_ref[...] += gdown_in[...].astype(F32)
    g_up.wait_recv()
    gup_ref[...] += gup_in[...].astype(F32)
    for copy in [w_up, w_down, g_up, g_down]:
        copy.wait_send()
    for group in gathers + scatters + gathers_b + scatters_b:
        for copy in group:
            copy.wait_send()


def on_device(tokens, w_up, w_down, cotangent):
    count, _, width = tokens.shape
    own = w_up.shape[2]
    n_token = lax.axis_size("token")
    head = width // n_token
    samples = CHUNKS * WIDE
    vmem = pl.BlockSpec(memory_space=pltpu.VMEM)

    def blocks(dtype):
        return pltpu.VMEM((CHUNKS, width, LANES), dtype)

    def scatter_scratch():
        return [
            pltpu.VMEM((width, samples), BF16),
            pltpu.VMEM((CHUNKS, width, 2 * LANES), BF16),
            blocks(BF16),
            blocks(BF16),
        ]

    output, grad_tokens, grad_up, grad_down = pl.pallas_call(
        functools.partial(kernel, n_token, head),
        out_shape=(
            jax.ShapeDtypeStruct((count, width), BF16),
            jax.ShapeDtypeStruct((count, width), BF16),
            jax.ShapeDtypeStruct((width, own), F32),
            jax.ShapeDtypeStruct((own, width), F32),
        ),
        in_specs=[vmem] * 4,
        out_specs=(vmem,) * 4,
        scratch_shapes=[
            blocks(BF16), blocks(BF16), blocks(BF16),
            pltpu.VMEM((width, own), BF16), pltpu.VMEM((own, width), BF16),
            pltpu.VMEM((2 * own, width), BF16), pltpu.VMEM((width, 2 * own), BF16),
            pltpu.VMEM((width, samples), BF16),
            pltpu.VMEM((2 * own, samples), BF16), pltpu.VMEM((2 * own, samples), BF16),
            pltpu.VMEM((width, samples), BF16),
            pltpu.VMEM((2 * own, samples), BF16),
            *scatter_scratch(), *scatter_scratch(),
            blocks(F32), pltpu.VMEM((CHUNKS, 8, LANES), F32), blocks(F32), blocks(F32), blocks(BF16), blocks(BF16),
            pltpu.VMEM((width, own), BF16), pltpu.VMEM((width, own), BF16),
            pltpu.VMEM((own, width), BF16), pltpu.VMEM((own, width), BF16),
            pltpu.SemaphoreType.DMA((COPIES,)), pltpu.SemaphoreType.DMA((COPIES,)),
        ],
        compiler_params=pltpu.CompilerParams(
            collective_id=0, has_side_effects=True, vmem_limit_bytes=58 * 1024 * 1024
        ),
        name="rankmixer",
    )(tokens[:, 0], w_up[0], w_down[0], cotangent[:, 0])
    return output[:, None], grad_tokens[:, None], grad_up[None], grad_down[None]


def solution(mesh):
    specs = (
        P("dp", "token", None),
        P("token", None, "dp"),
        P("token", "dp", None),
    )
    in_specs = specs + (specs[0],)
    out_specs = (specs[0], specs[0], specs[1], specs[2])
    return jax.shard_map(
        on_device, mesh=mesh, in_specs=in_specs, out_specs=out_specs, check_vma=False
    )
```

```python
import functools

import jax
import jax.numpy as jnp
from jax import lax
from jax.experimental import pallas as pl
from jax.experimental.pallas import tpu as pltpu
from jax.sharding import PartitionSpec as P

MESH = pl.DeviceIdType.MESH
EPSILON = 1e-05
CHUNKS = 2
LANES = 128
GROUP = 4
WIDE = GROUP * LANES
MXU_ROWS = 256
F32 = jnp.float32
BF16 = jnp.bfloat16

BLOCKS = 4

SPAN = CHUNKS * BLOCKS
MIX, MIX_BACK, UP, GRAD_DOWN, NEAR_Y, NEAR_Y_BACK, SHARED, HIDDEN = 0, 2, 4, 5, 6, 8, 10, 12
DOWN = 14
GATHER = DOWN + BLOCKS
SCATTER = GATHER + 2 * SPAN
GATHER_BACK = SCATTER + 2 * SPAN
SCATTER_BACK = GATHER_BACK + 2 * SPAN
COPIES = SCATTER_BACK + 2 * SPAN


def dot_nn(a, b):
    return jnp.dot(a, b, preferred_element_type=F32)


def dot_nt(a, b):
    return lax.dot_general(a, b, (((1,), (1,)), ((), ())), preferred_element_type=F32)


def layer_norm(values):
    centred = values - jnp.mean(values, axis=0, keepdims=True)
    scaling = lax.rsqrt(jnp.mean(centred * centred, axis=0, keepdims=True) + EPSILON)
    return centred * scaling, scaling


def norm_back(normed, scaling, upstream):
    first = jnp.mean(upstream, axis=0, keepdims=True)
    second = jnp.mean(upstream * normed, axis=0, keepdims=True)
    return scaling * (upstream - first - normed * second)


def gelu_and_slope(v):
    root = 0.7978845608028654
    square = v * v
    t = jnp.tanh(v * (root + (root * 0.044715) * square))
    half = 0.5 * (1.0 + t)
    inner = root + (3.0 * root * 0.044715) * square
    slope = half + (0.5 * v) * (1.0 - t * t) * inner
    return v * half, slope


def kernel(
    n_token, head,
    tok_ref, up_ref, down_ref, cot_ref,
    out_ref, gtok_ref, gup_ref, gdown_ref,
    tok_t, mixed, cot_t, up_far, down_far, up_t, down_t,
    shared, activ, slope, gffn, ghid,
    part_f, near_f, passed_f, far_f, part_b, near_b, passed_b, far_b,
    normed, scale_in, gout, gsum, gsum16, mixed_back,
    shared_far, ghid_far, gdown_out, gdown_in,
    send, recv,
):
    dp = lax.axis_index("dp")
    me = lax.axis_index("token")
    y, zh = dp // 2, dp % 2
    dev_y = ((y + 1 - 2 * (y % 2)) * 2 + zh, me)
    dev_z = (y * 2 + 1 - zh, me)
    dev_w = ((3 - y) * 2 + zh, me)
    d_model, own = up_ref.shape

    def remote(src, dst, sem, device):
        return pltpu.make_async_remote_copy(
            src_ref=src, dst_ref=dst, send_sem=send.at[sem], recv_sem=recv.at[sem],
            device_id=device, device_id_type=MESH,
        )

    block = d_model // BLOCKS

    def rows(i, n):
        return pl.ds(i * n if isinstance(i, int) else pl.multiple_of(i * n, n), n)

    def piece(ref, c, p, n=1, q=None):
        r = slice(None) if q is None else rows(q, block)
        return ref.at[r, pl.ds(c * WIDE + p * LANES, n * LANES)]

    barrier = pltpu.get_barrier_semaphore()

    @pl.loop(1, n_token)
    def _(i):
        pl.semaphore_signal(barrier, inc=1, device_id=(dp, (me + i) % n_token), device_id_type=MESH)

    for device in (dev_y, dev_z, dev_w):
        pl.semaphore_signal(barrier, inc=1, device_id=device, device_id_type=MESH)

    @pl.loop(0, d_model // LANES)
    def _(i):
        block = tok_ref[:, rows(i, LANES)].T
        for c in range(CHUNKS):
            tok_t[c, rows(i, LANES), :] = block[:, c * LANES:(c + 1) * LANES]

    pl.semaphore_wait(barrier, n_token + 2)

    def w_up():
        return remote(up_ref, up_far, UP, dev_w)

    def w_down(q):
        r = rows(q, block)
        return remote(down_ref.at[:, r], down_far.at[:, r], DOWN + q, dev_w)

    def shared_on(c):
        span = pl.ds(c * WIDE, WIDE)
        return remote(shared.at[:, span], shared_far.at[:, span], SHARED + c, dev_w)

    def hidden_on(c):
        span = pl.ds(c * WIDE, WIDE)
        return remote(ghid.at[pl.ds(own, own), span], ghid_far.at[:, span], HIDDEN + c, dev_w)

    def g_down():
        return remote(gdown_out, gdown_in, GRAD_DOWN, dev_w)

    def mix_start(src, dst, sem, c):
        @pl.loop(1, n_token)
        def _(i):
            to = (me + i) % n_token
            remote(
                src.at[c, rows(to, head), :], dst.at[c, rows(me, head), :], sem + c, (dp, to)
            ).start()

        dst[c, rows(me, head), :] = src[c, rows(me, head), :]

    def mix_wait(src, dst, sem, c):
        span = pl.ds(0, (n_token - 1) * head)
        whole = remote(src.at[c, span, :], dst.at[c, span, :], sem + c, dev_y)
        whole.wait_send()
        whole.wait_recv()

    def gather_y(ref, sem, c):
        return remote(piece(ref, c, 0), piece(ref, c, 2), sem + c, dev_y)

    def gather_z(ref, sem, c, q):
        return remote(piece(ref, c, 0, 1, q), piece(ref, c, 1, 1, q), sem + c * BLOCKS + q, dev_z)

    def gather_on(ref, sem, c, q):
        return remote(piece(ref, c, 1, 1, q), piece(ref, c, 3, 1, q), sem + SPAN + c * BLOCKS + q, dev_y)

    def scatter_y(part, near, sem, c, q):
        return remote(piece(part, c, 2, 2, q), near.at[c, rows(q, block), :], sem + c * BLOCKS + q, dev_y)

    def scatter_z(passed, far, sem, c, q):
        r = rows(q, block)
        return remote(passed.at[c, r, :], far.at[c, r, :], sem + SPAN + c * BLOCKS + q, dev_z)

    def each_block(step):
        pl.loop(0, BLOCKS)(step)

    def transpose_up(src, half):
        @pl.loop(0, own // LANES)
        def _(i):
            up_t[pl.ds(pl.multiple_of(half * own + i * LANES, LANES), LANES), :] = src[:, rows(i, LANES)].T

    def transpose_down(src, half, q):
        for i in range(block // LANES):
            r = pl.ds(q * block + i * LANES, LANES)
            down_t[r, pl.ds(half * own, own)] = src[:, r].T

    def norm_in(c):
        summed = mixed[c].astype(F32) + tok_t[c].astype(F32)
        value, scaling = layer_norm(summed)
        normed[c] = value
        scale_in[c, 0:1, :] = scaling
        shared[:, c * WIDE:c * WIDE + LANES] = value.astype(BF16)

    def up(c):
        span = pl.ds(c * WIDE, WIDE)

        @pl.loop(0, 2 * own // MXU_ROWS)
        def _(i):
            r = rows(i, MXU_ROWS)
            hidden = dot_nn(up_t[r, :], shared[:, span])
            value, grade = gelu_and_slope(hidden)
            activ[r, span] = value.astype(BF16)
            slope[r, span] = grade.astype(BF16)

    def down(c, q):
        r = rows(q, block)
        for p in (2, 0):
            span = pl.ds(c * WIDE + p * LANES, 2 * LANES)
            part_f[r, span] = dot_nn(down_t[r, :], activ[:, span]).astype(BF16)
            if p == 2:
                scatter_y(part_f, near_f, SCATTER, c, q).start()

    def pass_on(part, near, passed, far, sem, c, q):
        r = rows(q, block)
        scatter_y(part, near, sem, c, q).wait_recv()
        passed[c, r, :] = (
            part[r, c * WIDE + LANES:c * WIDE + 2 * LANES].astype(F32) + near[c, r, LANES:].astype(F32)
        ).astype(BF16)
        scatter_z(passed, far, sem, c, q).start()

    def total(part, near, far, c):
        return (
            part[:, c * WIDE:c * WIDE + LANES].astype(F32)
            + near[c, :, :LANES].astype(F32)
            + far[c].astype(F32)
        )

    def norm_out(c):
        ffn = total(part_f, near_f, far_f, c)
        value, scaling = layer_norm(ffn + shared[:, c * WIDE:c * WIDE + LANES].astype(F32))
        part_f[:, c * WIDE:c * WIDE + LANES] = value.astype(BF16)
        grad = norm_back(value, scaling, cot_t[c].astype(F32))
        gout[c] = grad
        gffn[:, c * WIDE:c * WIDE + LANES] = grad.astype(BF16)

    def write_out(c):
        @pl.loop(0, d_model // LANES)
        def _(i):
            out_ref[pl.ds(c * LANES, LANES), rows(i, LANES)] = part_f[rows(i, LANES), pl.ds(c * WIDE, LANES)].T

    def hidden_back(c):
        span = pl.ds(c * WIDE, WIDE)
        for half, src in enumerate((down_ref, down_far)):
            @pl.loop(0, own // MXU_ROWS)
            def _(i):
                r = pl.ds(pl.multiple_of(half * own + i * MXU_ROWS, MXU_ROWS), MXU_ROWS)
                grad = dot_nn(src[rows(i, MXU_ROWS), :], gffn[:, span])
                ghid[r, span] = (grad * slope[r, span].astype(F32)).astype(BF16)

    def shared_back(c, q):
        r = rows(q, block)
        for p in (2, 0):
            span = pl.ds(c * WIDE + p * LANES, 2 * LANES)
            part_b[r, span] = (
                dot_nn(up_ref[r, :], ghid[pl.ds(0, own), span])
                + dot_nn(up_far[r, :], ghid[pl.ds(own, own), span])
            ).astype(BF16)
            if p == 2:
                scatter_y(part_b, near_b, SCATTER_BACK, c, q).start()

    def sum_back(c):
        grad = total(part_b, near_b, far_b, c) + gout[c]
        grad = norm_back(normed[c], scale_in[c, 0:1, :], grad)
        gsum[c] = grad
        gsum16[c] = grad.astype(BF16)

    def tokens_back(c):
        @pl.loop(0, d_model // LANES)
        def _(i):
            r = rows(i, LANES)
            value = (gsum[c, r, :] + mixed_back[c, r, :].astype(F32)).astype(BF16)
            gtok_ref[pl.ds(c * LANES, LANES), r] = value.T

    def grad_down(half, dst):
        @pl.loop(0, own // MXU_ROWS)
        def _(i):
            r = pl.ds(pl.multiple_of(half * own + i * MXU_ROWS, MXU_ROWS), MXU_ROWS)
            dst[rows(i, MXU_ROWS), :] = dot_nt(activ[r, :], gffn[...]).astype(dst.dtype)

    def grad_up():
        @pl.loop(0, d_model // MXU_ROWS)
        def _(i):
            r = rows(i, MXU_ROWS)
            gup_ref[r, :] = dot_nt(shared[r, :], ghid[pl.ds(0, own), :]) + dot_nt(
                shared_far[r, pl.ds(0, WIDE)], ghid_far[:, pl.ds(0, WIDE)]
            )

    def grad_up_end():
        @pl.loop(0, d_model // MXU_ROWS)
        def _(i):
            r = rows(i, MXU_ROWS)
            gup_ref[r, :] += dot_nt(shared_far[r, pl.ds(WIDE, WIDE)], ghid_far[:, pl.ds(WIDE, WIDE)])

    for c in range(CHUNKS):
        mix_start(tok_t, mixed, MIX, c)
    w_up().start()
    for q in range(BLOCKS):
        w_down(q).start()
    transpose_up(up_ref, 0)
    for q in range(BLOCKS):
        transpose_down(down_ref, 0, q)

    @pl.loop(0, d_model // LANES)
    def _(i):
        tile = cot_ref[:, rows(i, LANES)].T
        for c in range(CHUNKS):
            cot_t[c, rows(i, LANES), :] = tile[:, c * LANES:(c + 1) * LANES]

    mix_wait(tok_t, mixed, MIX, 0)
    norm_in(0)
    gather_y(shared, NEAR_Y, 0).start()
    mix_wait(tok_t, mixed, MIX, 1)
    each_block(lambda q: gather_z(shared, GATHER, 0, q).start())
    norm_in(1)
    gather_y(shared, NEAR_Y, 1).start()

    def gather_turn(ref, sem):
        def step(q):
            gather_z(ref, sem, 0, q).wait_recv()
            gather_on(ref, sem, 0, q).start()
            gather_z(ref, sem, 1, q).start()

        each_block(step)

    def gather_end(ref, sem, near, c):
        gather_y(ref, near, c).wait_recv()
        each_block(lambda q: gather_on(ref, sem, c, q).wait_recv())

    def forward_on(ref, sem, q):
        gather_z(ref, sem, 1, q).wait_recv()
        gather_on(ref, sem, 1, q).start()

    def down_block(q):
        w_down(q).wait_recv()
        transpose_down(down_far, 1, q)
        down(0, q)

    def pass_f(c, q):
        pass_on(part_f, near_f, passed_f, far_f, SCATTER, c, q)

    def pass_b(c, q):
        pass_on(part_b, near_b, passed_b, far_b, SCATTER_BACK, c, q)

    gather_turn(shared, GATHER)
    w_up().wait_recv()
    transpose_up(up_far, 1)
    gather_end(shared, GATHER, NEAR_Y, 0)
    shared_on(0).start()
    up(0)
    down_block(0)
    forward_on(shared, GATHER, 0)
    forward_on(shared, GATHER, 1)
    down_block(1)
    forward_on(shared, GATHER, 2)
    forward_on(shared, GATHER, 3)
    pass_f(0, 0)
    gather_end(shared, GATHER, NEAR_Y, 1)
    shared_on(1).start()
    up(1)
    pass_f(0, 1)
    down_block(2)
    down(1, 0)
    down(1, 1)
    pass_f(0, 2)
    down(1, 2)
    down_block(3)
    pass_f(1, 0)
    down(1, 3)
    pass_f(0, 3)
    pass_f(1, 1)
    pass_f(1, 2)
    pass_f(1, 3)
    each_block(lambda q: scatter_z(passed_f, far_f, SCATTER, 0, q).wait_recv())
    norm_out(0)
    gather_y(gffn, NEAR_Y_BACK, 0).start()
    each_block(lambda q: gather_z(gffn, GATHER_BACK, 0, q).start())
    each_block(lambda q: scatter_z(passed_f, far_f, SCATTER, 1, q).wait_recv())
    norm_out(1)
    gather_y(gffn, NEAR_Y_BACK, 1).start()
    write_out(0)
    gather_turn(gffn, GATHER_BACK)
    write_out(1)
    gather_end(gffn, GATHER_BACK, NEAR_Y_BACK, 0)
    hidden_back(0)
    hidden_on(0).start()

    def back_block(q):
        shared_back(0, q)
        forward_on(gffn, GATHER_BACK, q)

    each_block(back_block)
    each_block(lambda q: pass_b(0, q))
    gather_end(gffn, GATHER_BACK, NEAR_Y_BACK, 1)
    grad_down(1, gdown_out)
    g_down().start()
    hidden_back(1)
    hidden_on(1).start()
    each_block(lambda q: shared_back(1, q))
    each_block(lambda q: pass_b(1, q))
    each_block(lambda q: scatter_z(passed_b, far_b, SCATTER_BACK, 0, q).wait_recv())
    sum_back(0)
    mix_start(gsum16, mixed_back, MIX_BACK, 0)
    grad_down(0, gdown_ref)
    each_block(lambda q: scatter_z(passed_b, far_b, SCATTER_BACK, 1, q).wait_recv())
    sum_back(1)
    mix_start(gsum16, mixed_back, MIX_BACK, 1)
    for c in range(CHUNKS):
        shared_on(c).wait_recv()
    hidden_on(0).wait_recv()
    grad_up()
    for c in range(CHUNKS):
        mix_wait(gsum16, mixed_back, MIX_BACK, c)
        tokens_back(c)
    g_down().wait_recv()
    gdown_ref[...] += gdown_in[...].astype(F32)
    hidden_on(1).wait_recv()
    grad_up_end()
    for copy in [w_up(), g_down(), shared_on(0), shared_on(1), hidden_on(0), hidden_on(1)]:
        copy.wait_send()
    each_block(lambda q: w_down(q).wait_send())
    for c in range(CHUNKS):
        gather_y(shared, NEAR_Y, c).wait_send()
        gather_y(gffn, NEAR_Y_BACK, c).wait_send()

        def drain(q):
            gather_z(shared, GATHER, c, q).wait_send()
            gather_on(shared, GATHER, c, q).wait_send()
            scatter_y(part_f, near_f, SCATTER, c, q).wait_send()
            scatter_z(passed_f, far_f, SCATTER, c, q).wait_send()
            gather_z(gffn, GATHER_BACK, c, q).wait_send()
            gather_on(gffn, GATHER_BACK, c, q).wait_send()
            scatter_y(part_b, near_b, SCATTER_BACK, c, q).wait_send()
            scatter_z(passed_b, far_b, SCATTER_BACK, c, q).wait_send()

        each_block(drain)


def on_device(tokens, w_up, w_down, cotangent):
    count, _, width = tokens.shape
    own = w_up.shape[2]
    n_token = lax.axis_size("token")
    head = width // n_token
    samples = CHUNKS * WIDE
    vmem = pl.BlockSpec(memory_space=pltpu.VMEM)

    def blocks(dtype):
        return pltpu.VMEM((CHUNKS, width, LANES), dtype)

    def scatter_scratch():
        return [
            pltpu.VMEM((width, samples), BF16),
            pltpu.VMEM((CHUNKS, width, 2 * LANES), BF16),
            blocks(BF16),
            blocks(BF16),
        ]

    output, grad_tokens, grad_up, grad_down = pl.pallas_call(
        functools.partial(kernel, n_token, head),
        out_shape=(
            jax.ShapeDtypeStruct((count, width), BF16),
            jax.ShapeDtypeStruct((count, width), BF16),
            jax.ShapeDtypeStruct((width, own), F32),
            jax.ShapeDtypeStruct((own, width), F32),
        ),
        in_specs=[vmem] * 4,
        out_specs=(vmem,) * 4,
        scratch_shapes=[
            blocks(BF16), blocks(BF16), blocks(BF16),
            pltpu.VMEM((width, own), BF16), pltpu.VMEM((own, width), BF16),
            pltpu.VMEM((2 * own, width), BF16), pltpu.VMEM((width, 2 * own), BF16),
            pltpu.VMEM((width, samples), BF16),
            pltpu.VMEM((2 * own, samples), BF16), pltpu.VMEM((2 * own, samples), BF16),
            pltpu.VMEM((width, samples), BF16),
            pltpu.VMEM((2 * own, samples), BF16),
            *scatter_scratch(), *scatter_scratch(),
            blocks(F32), pltpu.VMEM((CHUNKS, 8, LANES), F32), blocks(F32), blocks(F32), blocks(BF16), blocks(BF16),
            pltpu.VMEM((width, samples), BF16), pltpu.VMEM((own, samples), BF16),
            pltpu.VMEM((own, width), BF16), pltpu.VMEM((own, width), BF16),
            pltpu.SemaphoreType.DMA((COPIES,)), pltpu.SemaphoreType.DMA((COPIES,)),
        ],
        compiler_params=pltpu.CompilerParams(
            collective_id=0, has_side_effects=True, vmem_limit_bytes=58 * 1024 * 1024
        ),
        name="rankmixer",
    )(tokens[:, 0], w_up[0], w_down[0], cotangent[:, 0])
    return output[:, None], grad_tokens[:, None], grad_up[None], grad_down[None]


def solution(mesh):
    specs = (
        P("dp", "token", None),
        P("token", None, "dp"),
        P("token", "dp", None),
    )
    in_specs = specs + (specs[0],)
    out_specs = (specs[0], specs[0], specs[1], specs[2])
    return jax.shard_map(
        on_device, mesh=mesh, in_specs=in_specs, out_specs=out_specs, check_vma=False
    )
```

```python
import functools

import jax
import jax.numpy as jnp
from jax import lax
from jax.experimental import pallas as pl
from jax.experimental.pallas import tpu as pltpu
from jax.sharding import PartitionSpec as P

MESH = pl.DeviceIdType.MESH
EPSILON = 1e-05
CHUNKS = 2
LANES = 128
GROUP = 4
WIDE = GROUP * LANES
MXU_ROWS = 256
F32 = jnp.float32
BF16 = jnp.bfloat16

BLOCKS = 4

SPAN = CHUNKS * BLOCKS
MIX, MIX_BACK, UP, GRAD_DOWN, NEAR_Y, NEAR_Y_BACK, SHARED, HIDDEN = 0, 2, 4, 5, 6, 8, 10, 12
DOWN = 14
GATHER = DOWN + BLOCKS
SCATTER = GATHER + 2 * SPAN
GATHER_BACK = SCATTER + 2 * SPAN
SCATTER_BACK = GATHER_BACK + 2 * SPAN
COPIES = SCATTER_BACK + 2 * SPAN


def dot_nn(a, b):
    return jnp.dot(a, b, preferred_element_type=F32)


def dot_nt(a, b):
    return lax.dot_general(a, b, (((1,), (1,)), ((), ())), preferred_element_type=F32)


def layer_norm(values):
    centred = values - jnp.mean(values, axis=0, keepdims=True)
    scaling = lax.rsqrt(jnp.mean(centred * centred, axis=0, keepdims=True) + EPSILON)
    return centred * scaling, scaling


def norm_back(normed, scaling, upstream):
    first = jnp.mean(upstream, axis=0, keepdims=True)
    second = jnp.mean(upstream * normed, axis=0, keepdims=True)
    return scaling * (upstream - first - normed * second)


def gelu_and_slope(v):
    root = 0.7978845608028654
    square = v * v
    t = jnp.tanh(v * (root + (root * 0.044715) * square))
    half = 0.5 * (1.0 + t)
    inner = root + (3.0 * root * 0.044715) * square
    slope = half + (0.5 * v) * (1.0 - t * t) * inner
    return v * half, slope


def kernel(
    n_token, head,
    tok_ref, up_ref, down_ref, cot_ref,
    out_ref, gtok_ref, gup_ref, gdown_ref,
    tok_t, mixed, cot_t, up_far, down_far, up_t, down_t,
    shared, activ, slope, gffn, ghid,
    part_f, near_f, passed_f, far_f, part_b, near_b, passed_b, far_b,
    normed, scale_in, gout, gsum, gsum16, mixed_back,
    shared_far, ghid_far, gdown_out, gdown_in,
    send, recv,
):
    dp = lax.axis_index("dp")
    me = lax.axis_index("token")
    y, zh = dp // 2, dp % 2
    dev_y = ((y + 1 - 2 * (y % 2)) * 2 + zh, me)
    dev_z = (y * 2 + 1 - zh, me)
    dev_w = ((3 - y) * 2 + zh, me)
    d_model, own = up_ref.shape

    def remote(src, dst, sem, device):
        return pltpu.make_async_remote_copy(
            src_ref=src, dst_ref=dst, send_sem=send.at[sem], recv_sem=recv.at[sem],
            device_id=device, device_id_type=MESH,
        )

    block = d_model // BLOCKS

    def rows(i, n):
        return pl.ds(i * n if isinstance(i, int) else pl.multiple_of(i * n, n), n)

    def piece(ref, c, p, n=1, q=None):
        r = slice(None) if q is None else rows(q, block)
        return ref.at[r, pl.ds(c * WIDE + p * LANES, n * LANES)]

    barrier = pltpu.get_barrier_semaphore()

    @pl.loop(1, n_token)
    def _(i):
        pl.semaphore_signal(barrier, inc=1, device_id=(dp, (me + i) % n_token), device_id_type=MESH)

    for device in (dev_y, dev_z, dev_w):
        pl.semaphore_signal(barrier, inc=1, device_id=device, device_id_type=MESH)

    @pl.loop(0, d_model // LANES)
    def _(i):
        block = tok_ref[:, rows(i, LANES)].T
        for c in range(CHUNKS):
            tok_t[c, rows(i, LANES), :] = block[:, c * LANES:(c + 1) * LANES]

    pl.semaphore_wait(barrier, n_token + 2)

    def w_up():
        return remote(up_ref, up_far, UP, dev_w)

    def w_down(q):
        r = rows(q, block)
        return remote(down_ref.at[:, r], down_far.at[:, r], DOWN + q, dev_w)

    def shared_on(c):
        span = pl.ds(c * WIDE, WIDE)
        return remote(shared.at[:, span], shared_far.at[:, span], SHARED + c, dev_w)

    def hidden_on(c):
        span = pl.ds(c * WIDE, WIDE)
        return remote(ghid.at[pl.ds(own, own), span], ghid_far.at[:, span], HIDDEN + c, dev_w)

    def g_down():
        return remote(gdown_out, gdown_in, GRAD_DOWN, dev_w)

    def mix_start(src, dst, sem, c):
        @pl.loop(1, n_token)
        def _(i):
            to = (me + i) % n_token
            remote(
                src.at[c, rows(to, head), :], dst.at[c, rows(me, head), :], sem + c, (dp, to)
            ).start()

        dst[c, rows(me, head), :] = src[c, rows(me, head), :]

    def mix_wait(src, dst, sem, c):
        span = pl.ds(0, (n_token - 1) * head)
        whole = remote(src.at[c, span, :], dst.at[c, span, :], sem + c, dev_y)
        whole.wait_send()
        whole.wait_recv()

    def gather_y(ref, sem, c):
        return remote(piece(ref, c, 0), piece(ref, c, 2), sem + c, dev_y)

    def gather_z(ref, sem, c, q):
        return remote(piece(ref, c, 0, 1, q), piece(ref, c, 1, 1, q), sem + c * BLOCKS + q, dev_z)

    def gather_on(ref, sem, c, q):
        return remote(piece(ref, c, 1, 1, q), piece(ref, c, 3, 1, q), sem + SPAN + c * BLOCKS + q, dev_y)

    def scatter_y(part, near, sem, c, q):
        return remote(piece(part, c, 2, 2, q), near.at[c, rows(q, block), :], sem + c * BLOCKS + q, dev_y)

    def scatter_z(passed, far, sem, c, q):
        r = rows(q, block)
        return remote(passed.at[c, r, :], far.at[c, r, :], sem + SPAN + c * BLOCKS + q, dev_z)

    def each_block(step):
        pl.loop(0, BLOCKS)(step)

    def transpose_up(src, half):
        @pl.loop(0, own // LANES)
        def _(i):
            up_t[pl.ds(pl.multiple_of(half * own + i * LANES, LANES), LANES), :] = src[:, rows(i, LANES)].T

    def transpose_down(src, half, q):
        for i in range(block // LANES):
            r = pl.ds(q * block + i * LANES, LANES)
            down_t[r, pl.ds(half * own, own)] = src[:, r].T

    def norm_in(c):
        summed = mixed[c].astype(F32) + tok_t[c].astype(F32)
        value, scaling = layer_norm(summed)
        normed[c] = value
        scale_in[c, 0:1, :] = scaling
        shared[:, c * WIDE:c * WIDE + LANES] = value.astype(BF16)

    def up(c):
        span = pl.ds(c * WIDE, WIDE)

        @pl.loop(0, 2 * own // MXU_ROWS)
        def _(i):
            r = rows(i, MXU_ROWS)
            hidden = dot_nn(up_t[r, :], shared[:, span])
            value, grade = gelu_and_slope(hidden)
            activ[r, span] = value.astype(BF16)
            slope[r, span] = grade.astype(BF16)

    def down(c, q):
        r = rows(q, block)
        for p in (2, 0):
            span = pl.ds(c * WIDE + p * LANES, 2 * LANES)
            part_f[r, span] = dot_nn(down_t[r, :], activ[:, span]).astype(BF16)
            if p == 2:
                scatter_y(part_f, near_f, SCATTER, c, q).start()

    def pass_on(part, near, passed, far, sem, c, q):
        r = rows(q, block)
        scatter_y(part, near, sem, c, q).wait_recv()
        passed[c, r, :] = (
            part[r, c * WIDE + LANES:c * WIDE + 2 * LANES].astype(F32) + near[c, r, LANES:].astype(F32)
        ).astype(BF16)
        scatter_z(passed, far, sem, c, q).start()

    def total(part, near, far, c):
        return (
            part[:, c * WIDE:c * WIDE + LANES].astype(F32)
            + near[c, :, :LANES].astype(F32)
            + far[c].astype(F32)
        )

    def norm_out(c):
        ffn = total(part_f, near_f, far_f, c)
        value, scaling = layer_norm(ffn + shared[:, c * WIDE:c * WIDE + LANES].astype(F32))
        part_f[:, c * WIDE:c * WIDE + LANES] = value.astype(BF16)
        grad = norm_back(value, scaling, cot_t[c].astype(F32))
        gout[c] = grad
        gffn[:, c * WIDE:c * WIDE + LANES] = grad.astype(BF16)

    def write_out(c):
        @pl.loop(0, d_model // LANES)
        def _(i):
            out_ref[pl.ds(c * LANES, LANES), rows(i, LANES)] = part_f[rows(i, LANES), pl.ds(c * WIDE, LANES)].T

    def hidden_back(c):
        span = pl.ds(c * WIDE, WIDE)
        for half, src in enumerate((down_ref, down_far)):
            @pl.loop(0, own // MXU_ROWS)
            def _(i):
                r = pl.ds(pl.multiple_of(half * own + i * MXU_ROWS, MXU_ROWS), MXU_ROWS)
                grad = dot_nn(src[rows(i, MXU_ROWS), :], gffn[:, span])
                ghid[r, span] = (grad * slope[r, span].astype(F32)).astype(BF16)

    def shared_back(c, q):
        r = rows(q, block)
        for p in (2, 0):
            span = pl.ds(c * WIDE + p * LANES, 2 * LANES)
            part_b[r, span] = (
                dot_nn(up_ref[r, :], ghid[pl.ds(0, own), span])
                + dot_nn(up_far[r, :], ghid[pl.ds(own, own), span])
            ).astype(BF16)
            if p == 2:
                scatter_y(part_b, near_b, SCATTER_BACK, c, q).start()

    def sum_back(c):
        grad = total(part_b, near_b, far_b, c) + gout[c]
        grad = norm_back(normed[c], scale_in[c, 0:1, :], grad)
        gsum[c] = grad
        gsum16[c] = grad.astype(BF16)

    def tokens_back(c):
        @pl.loop(0, d_model // LANES)
        def _(i):
            r = rows(i, LANES)
            value = (gsum[c, r, :] + mixed_back[c, r, :].astype(F32)).astype(BF16)
            gtok_ref[pl.ds(c * LANES, LANES), r] = value.T

    def grad_down(half, dst):
        @pl.loop(0, own // MXU_ROWS)
        def _(i):
            r = pl.ds(pl.multiple_of(half * own + i * MXU_ROWS, MXU_ROWS), MXU_ROWS)
            dst[rows(i, MXU_ROWS), :] = dot_nt(activ[r, :], gffn[...]).astype(dst.dtype)

    def grad_up():
        @pl.loop(0, d_model // MXU_ROWS)
        def _(i):
            r = rows(i, MXU_ROWS)
            gup_ref[r, :] = dot_nt(shared[r, :], ghid[pl.ds(0, own), :]) + dot_nt(
                shared_far[r, pl.ds(0, WIDE)], ghid_far[:, pl.ds(0, WIDE)]
            )

    def grad_up_end():
        @pl.loop(0, d_model // MXU_ROWS)
        def _(i):
            r = rows(i, MXU_ROWS)
            gup_ref[r, :] += dot_nt(shared_far[r, pl.ds(WIDE, WIDE)], ghid_far[:, pl.ds(WIDE, WIDE)])

    for c in range(CHUNKS):
        mix_start(tok_t, mixed, MIX, c)
    w_up().start()
    for q in range(BLOCKS):
        w_down(q).start()
    transpose_up(up_ref, 0)
    for q in range(BLOCKS):
        transpose_down(down_ref, 0, q)

    @pl.loop(0, d_model // LANES)
    def _(i):
        tile = cot_ref[:, rows(i, LANES)].T
        for c in range(CHUNKS):
            cot_t[c, rows(i, LANES), :] = tile[:, c * LANES:(c + 1) * LANES]

    mix_wait(tok_t, mixed, MIX, 0)
    norm_in(0)
    gather_y(shared, NEAR_Y, 0).start()
    mix_wait(tok_t, mixed, MIX, 1)
    each_block(lambda q: gather_z(shared, GATHER, 0, q).start())
    norm_in(1)
    gather_y(shared, NEAR_Y, 1).start()

    def gather_turn(ref, sem):
        def step(q):
            gather_z(ref, sem, 0, q).wait_recv()
            gather_on(ref, sem, 0, q).start()
            gather_z(ref, sem, 1, q).start()

        each_block(step)

    def gather_end(ref, sem, near, c):
        gather_y(ref, near, c).wait_recv()
        each_block(lambda q: gather_on(ref, sem, c, q).wait_recv())

    def forward_on(ref, sem, q):
        gather_z(ref, sem, 1, q).wait_recv()
        gather_on(ref, sem, 1, q).start()

    def down_block(q):
        w_down(q).wait_recv()
        transpose_down(down_far, 1, q)
        down(0, q)

    def pass_f(c, q):
        pass_on(part_f, near_f, passed_f, far_f, SCATTER, c, q)

    def pass_b(c, q):
        pass_on(part_b, near_b, passed_b, far_b, SCATTER_BACK, c, q)

    gather_turn(shared, GATHER)
    w_up().wait_recv()
    transpose_up(up_far, 1)
    gather_end(shared, GATHER, NEAR_Y, 0)
    up(0)
    for q in range(BLOCKS - 1):
        down_block(q)
        forward_on(shared, GATHER, q)
    pass_f(0, 0)
    down_block(3)
    forward_on(shared, GATHER, 3)
    shared_on(0).start()
    pass_f(0, 1)
    pass_f(0, 2)
    gather_end(shared, GATHER, NEAR_Y, 1)
    shared_on(1).start()
    pass_f(0, 3)
    up(1)
    each_block(lambda q: down(1, q))
    each_block(lambda q: pass_f(1, q))
    each_block(lambda q: scatter_z(passed_f, far_f, SCATTER, 0, q).wait_recv())
    norm_out(0)
    gather_y(gffn, NEAR_Y_BACK, 0).start()
    each_block(lambda q: gather_z(gffn, GATHER_BACK, 0, q).start())
    each_block(lambda q: scatter_z(passed_f, far_f, SCATTER, 1, q).wait_recv())
    norm_out(1)
    gather_y(gffn, NEAR_Y_BACK, 1).start()
    write_out(0)
    gather_turn(gffn, GATHER_BACK)
    write_out(1)
    gather_end(gffn, GATHER_BACK, NEAR_Y_BACK, 0)
    hidden_back(0)
    hidden_on(0).start()

    def back_block(q):
        shared_back(0, q)
        forward_on(gffn, GATHER_BACK, q)

    each_block(back_block)
    each_block(lambda q: pass_b(0, q))
    gather_end(gffn, GATHER_BACK, NEAR_Y_BACK, 1)
    hidden_back(1)
    hidden_on(1).start()
    each_block(lambda q: shared_back(1, q))
    grad_down(1, gdown_out)
    g_down().start()
    pass_b(1, 0)
    each_block(lambda q: scatter_z(passed_b, far_b, SCATTER_BACK, 0, q).wait_recv())
    sum_back(0)
    mix_start(gsum16, mixed_back, MIX_BACK, 0)
    pl.loop(1, BLOCKS)(lambda q: pass_b(1, q))
    grad_down(0, gdown_ref)
    each_block(lambda q: scatter_z(passed_b, far_b, SCATTER_BACK, 1, q).wait_recv())
    sum_back(1)
    mix_start(gsum16, mixed_back, MIX_BACK, 1)
    for c in range(CHUNKS):
        shared_on(c).wait_recv()
    hidden_on(0).wait_recv()
    grad_up()
    hidden_on(1).wait_recv()
    grad_up_end()
    g_down().wait_recv()
    gdown_ref[...] += gdown_in[...].astype(F32)
    for c in range(CHUNKS):
        mix_wait(gsum16, mixed_back, MIX_BACK, c)
        tokens_back(c)
    for copy in [w_up(), g_down(), shared_on(0), shared_on(1), hidden_on(0), hidden_on(1)]:
        copy.wait_send()
    each_block(lambda q: w_down(q).wait_send())
    for c in range(CHUNKS):
        gather_y(shared, NEAR_Y, c).wait_send()
        gather_y(gffn, NEAR_Y_BACK, c).wait_send()

        def drain(q):
            gather_z(shared, GATHER, c, q).wait_send()
            gather_on(shared, GATHER, c, q).wait_send()
            scatter_y(part_f, near_f, SCATTER, c, q).wait_send()
            scatter_z(passed_f, far_f, SCATTER, c, q).wait_send()
            gather_z(gffn, GATHER_BACK, c, q).wait_send()
            gather_on(gffn, GATHER_BACK, c, q).wait_send()
            scatter_y(part_b, near_b, SCATTER_BACK, c, q).wait_send()
            scatter_z(passed_b, far_b, SCATTER_BACK, c, q).wait_send()

        each_block(drain)


def on_device(tokens, w_up, w_down, cotangent):
    count, _, width = tokens.shape
    own = w_up.shape[2]
    n_token = lax.axis_size("token")
    head = width // n_token
    samples = CHUNKS * WIDE
    vmem = pl.BlockSpec(memory_space=pltpu.VMEM)

    def blocks(dtype):
        return pltpu.VMEM((CHUNKS, width, LANES), dtype)

    def scatter_scratch():
        return [
            pltpu.VMEM((width, samples), BF16),
            pltpu.VMEM((CHUNKS, width, 2 * LANES), BF16),
            blocks(BF16),
            blocks(BF16),
        ]

    output, grad_tokens, grad_up, grad_down = pl.pallas_call(
        functools.partial(kernel, n_token, head),
        out_shape=(
            pltpu.VMEM((count, width), BF16),
            pltpu.VMEM((count, width), BF16),
            pltpu.VMEM((width, own), F32),
            pltpu.VMEM((own, width), F32),
        ),
        in_specs=[vmem] * 4,
        out_specs=(vmem,) * 4,
        scratch_shapes=[
            blocks(BF16), blocks(BF16), blocks(BF16),
            pltpu.VMEM((width, own), BF16), pltpu.VMEM((own, width), BF16),
            pltpu.VMEM((2 * own, width), BF16), pltpu.VMEM((width, 2 * own), BF16),
            pltpu.VMEM((width, samples), BF16),
            pltpu.VMEM((2 * own, samples), BF16), pltpu.VMEM((2 * own, samples), BF16),
            pltpu.VMEM((width, samples), BF16),
            pltpu.VMEM((2 * own, samples), BF16),
            *scatter_scratch(), *scatter_scratch(),
            blocks(F32), pltpu.VMEM((CHUNKS, 8, LANES), F32), blocks(F32), blocks(F32), blocks(BF16), blocks(BF16),
            pltpu.VMEM((width, samples), BF16), pltpu.VMEM((own, samples), BF16),
            pltpu.VMEM((own, width), BF16), pltpu.VMEM((own, width), BF16),
            pltpu.SemaphoreType.DMA((COPIES,)), pltpu.SemaphoreType.DMA((COPIES,)),
        ],
        compiler_params=pltpu.CompilerParams(
            collective_id=0, has_side_effects=True, vmem_limit_bytes=50 * 1024 * 1024
        ),
        name="rankmixer",
    )(tokens[:, 0], w_up[0], w_down[0], cotangent[:, 0])
    return output[:, None], grad_tokens[:, None], grad_up[None], grad_down[None]


def solution(mesh):
    specs = (
        P("dp", "token", None),
        P("token", None, "dp"),
        P("token", "dp", None),
    )
    in_specs = specs + (specs[0],)
    out_specs = (specs[0], specs[0], specs[1], specs[2])
    return jax.shard_map(
        on_device, mesh=mesh, in_specs=in_specs, out_specs=out_specs, check_vma=False
    )
```

```python
import functools

import jax
import jax.numpy as jnp
from jax import lax
from jax.experimental import pallas as pl
from jax.experimental.pallas import tpu as pltpu
from jax.sharding import PartitionSpec as P

MESH = pl.DeviceIdType.MESH
EPSILON = 1e-05
CHUNKS = 2
LANES = 128
GROUP = 4
WIDE = GROUP * LANES
MXU_ROWS = 256
F32 = jnp.float32
BF16 = jnp.bfloat16

BLOCKS = 4

SPAN = CHUNKS * BLOCKS
MIX, MIX_BACK, UP, GRAD_DOWN, NEAR_Y, NEAR_Y_BACK, SHARED, HIDDEN = 0, 2, 4, 5, 6, 8, 10, 12
SCATTER_OWN, SCATTER_OWN_BACK = 14, 16
DOWN = 18
GATHER = DOWN + BLOCKS
SCATTER = GATHER + 2 * SPAN
GATHER_BACK = SCATTER + 2 * SPAN
SCATTER_BACK = GATHER_BACK + 2 * SPAN
COPIES = SCATTER_BACK + 2 * SPAN


def dot_nn(a, b):
    return jnp.dot(a, b, preferred_element_type=F32)


def dot_nt(a, b):
    return lax.dot_general(a, b, (((1,), (1,)), ((), ())), preferred_element_type=F32)


def layer_norm(values):
    centred = values - jnp.mean(values, axis=0, keepdims=True)
    scaling = lax.rsqrt(jnp.mean(centred * centred, axis=0, keepdims=True) + EPSILON)
    return centred * scaling, scaling


def norm_back(normed, scaling, upstream):
    first = jnp.mean(upstream, axis=0, keepdims=True)
    second = jnp.mean(upstream * normed, axis=0, keepdims=True)
    return scaling * (upstream - first - normed * second)


def gelu_and_slope(v):
    root = 0.7978845608028654
    square = v * v
    t = jnp.tanh(v * (root + (root * 0.044715) * square))
    half = 0.5 * (1.0 + t)
    inner = root + (3.0 * root * 0.044715) * square
    slope = half + (0.5 * v) * (1.0 - t * t) * inner
    return v * half, slope


def kernel(
    n_token, head,
    tok_ref, up_ref, down_ref, cot_ref,
    out_ref, gtok_ref, gup_ref, gdown_ref,
    tok_t, mixed, cot_t, up_far, down_far, up_t, down_t,
    shared, activ, slope, gffn, ghid,
    part_f, near_f, passed_f, far_f, part_b, near_b, passed_b, far_b,
    normed, scale_in, gout, gsum, gsum16, mixed_back,
    shared_far, ghid_far, gdown_out, gdown_in,
    send, recv,
):
    dp = lax.axis_index("dp")
    me = lax.axis_index("token")
    y, zh = dp // 2, dp % 2
    dev_y = ((y + 1 - 2 * (y % 2)) * 2 + zh, me)
    dev_z = (y * 2 + 1 - zh, me)
    dev_w = ((3 - y) * 2 + zh, me)
    d_model, own = up_ref.shape

    def remote(src, dst, sem, device):
        return pltpu.make_async_remote_copy(
            src_ref=src, dst_ref=dst, send_sem=send.at[sem], recv_sem=recv.at[sem],
            device_id=device, device_id_type=MESH,
        )

    block = d_model // BLOCKS

    def rows(i, n):
        return pl.ds(i * n if isinstance(i, int) else pl.multiple_of(i * n, n), n)

    def piece(ref, c, p, n=1, q=None):
        r = slice(None) if q is None else rows(q, block)
        return ref.at[r, pl.ds(c * WIDE + p * LANES, n * LANES)]

    barrier = pltpu.get_barrier_semaphore()

    @pl.loop(1, n_token)
    def _(i):
        pl.semaphore_signal(barrier, inc=1, device_id=(dp, (me + i) % n_token), device_id_type=MESH)

    for device in (dev_y, dev_z, dev_w):
        pl.semaphore_signal(barrier, inc=1, device_id=device, device_id_type=MESH)

    @pl.loop(0, d_model // LANES)
    def _(i):
        block = tok_ref[:, rows(i, LANES)].T
        for c in range(CHUNKS):
            tok_t[c, rows(i, LANES), :] = block[:, c * LANES:(c + 1) * LANES]

    pl.semaphore_wait(barrier, n_token + 2)

    def w_up():
        return remote(up_ref, up_far, UP, dev_w)

    def w_down(q):
        r = rows(q, block)
        return remote(down_ref.at[:, r], down_far.at[:, r], DOWN + q, dev_w)

    def shared_on(c):
        span = pl.ds(c * WIDE, WIDE)
        return remote(shared.at[:, span], shared_far.at[:, span], SHARED + c, dev_w)

    def hidden_on(c):
        span = pl.ds(c * WIDE, WIDE)
        return remote(ghid.at[pl.ds(own, own), span], ghid_far.at[:, span], HIDDEN + c, dev_w)

    def g_down():
        return remote(gdown_out, gdown_in, GRAD_DOWN, dev_w)

    def mix_start(src, dst, sem, c):
        @pl.loop(1, n_token)
        def _(i):
            to = (me + i) % n_token
            remote(
                src.at[c, rows(to, head), :], dst.at[c, rows(me, head), :], sem + c, (dp, to)
            ).start()

        dst[c, rows(me, head), :] = src[c, rows(me, head), :]

    def mix_wait(src, dst, sem, c):
        span = pl.ds(0, (n_token - 1) * head)
        whole = remote(src.at[c, span, :], dst.at[c, span, :], sem + c, dev_y)
        whole.wait_send()
        whole.wait_recv()

    def gather_y(ref, sem, c):
        return remote(piece(ref, c, 0), piece(ref, c, 2), sem + c, dev_y)

    def gather_z(ref, sem, c, q):
        return remote(piece(ref, c, 0, 1, q), piece(ref, c, 1, 1, q), sem + c * BLOCKS + q, dev_z)

    def gather_on(ref, sem, c, q):
        return remote(piece(ref, c, 1, 1, q), piece(ref, c, 3, 1, q), sem + SPAN + c * BLOCKS + q, dev_y)

    def scatter_y(part, near, sem, c, q):
        r = rows(q, block)
        return remote(piece(part, c, 3, 1, q), near.at[c, r, pl.ds(LANES, LANES)], sem + c * BLOCKS + q, dev_y)

    def scatter_own(part, near, sem, c):
        return remote(piece(part, c, 2), near.at[c, :, pl.ds(0, LANES)], sem + c, dev_y)

    def scatter_z(passed, far, sem, c, q):
        r = rows(q, block)
        return remote(passed.at[c, r, :], far.at[c, r, :], sem + SPAN + c * BLOCKS + q, dev_z)

    def each_block(step):
        pl.loop(0, BLOCKS)(step)

    def transpose_up(src, half):
        @pl.loop(0, own // LANES)
        def _(i):
            up_t[pl.ds(pl.multiple_of(half * own + i * LANES, LANES), LANES), :] = src[:, rows(i, LANES)].T

    def transpose_down(src, half, q):
        for i in range(block // LANES):
            r = pl.ds(q * block + i * LANES, LANES)
            down_t[r, pl.ds(half * own, own)] = src[:, r].T

    def norm_in(c):
        summed = mixed[c].astype(F32) + tok_t[c].astype(F32)
        value, scaling = layer_norm(summed)
        normed[c] = value
        scale_in[c, 0:1, :] = scaling
        shared[:, c * WIDE:c * WIDE + LANES] = value.astype(BF16)

    def up(c):
        span = pl.ds(c * WIDE, WIDE)

        @pl.loop(0, 2 * own // MXU_ROWS)
        def _(i):
            r = rows(i, MXU_ROWS)
            hidden = dot_nn(up_t[r, :], shared[:, span])
            value, grade = gelu_and_slope(hidden)
            activ[r, span] = value.astype(BF16)
            slope[r, span] = grade.astype(BF16)

    def down(c, q):
        r = rows(q, block)
        for p in (2, 0):
            span = pl.ds(c * WIDE + p * LANES, 2 * LANES)
            part_f[r, span] = dot_nn(down_t[r, :], activ[:, span]).astype(BF16)
            if p == 2:
                scatter_y(part_f, near_f, SCATTER, c, q).start()

    def pass_on(part, near, passed, far, sem, c, q):
        r = rows(q, block)
        scatter_y(part, near, sem, c, q).wait_recv()
        passed[c, r, :] = (
            part[r, c * WIDE + LANES:c * WIDE + 2 * LANES].astype(F32) + near[c, r, LANES:].astype(F32)
        ).astype(BF16)
        scatter_z(passed, far, sem, c, q).start()

    def total(part, near, far, c):
        return (
            part[:, c * WIDE:c * WIDE + LANES].astype(F32)
            + near[c, :, :LANES].astype(F32)
            + far[c].astype(F32)
        )

    def norm_out(c):
        ffn = total(part_f, near_f, far_f, c)
        value, scaling = layer_norm(ffn + shared[:, c * WIDE:c * WIDE + LANES].astype(F32))
        part_f[:, c * WIDE:c * WIDE + LANES] = value.astype(BF16)
        grad = norm_back(value, scaling, cot_t[c].astype(F32))
        gout[c] = grad
        gffn[:, c * WIDE:c * WIDE + LANES] = grad.astype(BF16)

    def write_out(c):
        @pl.loop(0, d_model // LANES)
        def _(i):
            out_ref[pl.ds(c * LANES, LANES), rows(i, LANES)] = part_f[rows(i, LANES), pl.ds(c * WIDE, LANES)].T

    def hidden_back(c):
        span = pl.ds(c * WIDE, WIDE)
        for half, src in enumerate((down_ref, down_far)):
            @pl.loop(0, own // MXU_ROWS)
            def _(i):
                r = pl.ds(pl.multiple_of(half * own + i * MXU_ROWS, MXU_ROWS), MXU_ROWS)
                grad = dot_nn(src[rows(i, MXU_ROWS), :], gffn[:, span])
                ghid[r, span] = (grad * slope[r, span].astype(F32)).astype(BF16)

    def shared_back(c, q):
        r = rows(q, block)
        for p in (2, 0):
            span = pl.ds(c * WIDE + p * LANES, 2 * LANES)
            part_b[r, span] = (
                dot_nn(up_ref[r, :], ghid[pl.ds(0, own), span])
                + dot_nn(up_far[r, :], ghid[pl.ds(own, own), span])
            ).astype(BF16)
            if p == 2:
                scatter_y(part_b, near_b, SCATTER_BACK, c, q).start()

    def sum_back(c):
        grad = total(part_b, near_b, far_b, c) + gout[c]
        grad = norm_back(normed[c], scale_in[c, 0:1, :], grad)
        gsum[c] = grad
        gsum16[c] = grad.astype(BF16)

    def tokens_back(c):
        @pl.loop(0, d_model // LANES)
        def _(i):
            r = rows(i, LANES)
            value = (gsum[c, r, :] + mixed_back[c, r, :].astype(F32)).astype(BF16)
            gtok_ref[pl.ds(c * LANES, LANES), r] = value.T

    def grad_down(half, dst):
        @pl.loop(0, own // MXU_ROWS)
        def _(i):
            r = pl.ds(pl.multiple_of(half * own + i * MXU_ROWS, MXU_ROWS), MXU_ROWS)
            dst[rows(i, MXU_ROWS), :] = dot_nt(activ[r, :], gffn[...]).astype(dst.dtype)

    def grad_up():
        @pl.loop(0, d_model // MXU_ROWS)
        def _(i):
            r = rows(i, MXU_ROWS)
            gup_ref[r, :] = dot_nt(shared[r, :], ghid[pl.ds(0, own), :]) + dot_nt(
                shared_far[r, pl.ds(0, WIDE)], ghid_far[:, pl.ds(0, WIDE)]
            )

    def grad_up_end():
        @pl.loop(0, d_model // MXU_ROWS)
        def _(i):
            r = rows(i, MXU_ROWS)
            gup_ref[r, :] += dot_nt(shared_far[r, pl.ds(WIDE, WIDE)], ghid_far[:, pl.ds(WIDE, WIDE)])

    for c in range(CHUNKS):
        mix_start(tok_t, mixed, MIX, c)
    w_up().start()
    for q in range(BLOCKS):
        w_down(q).start()
    transpose_up(up_ref, 0)
    for q in range(BLOCKS):
        transpose_down(down_ref, 0, q)

    @pl.loop(0, d_model // LANES)
    def _(i):
        tile = cot_ref[:, rows(i, LANES)].T
        for c in range(CHUNKS):
            cot_t[c, rows(i, LANES), :] = tile[:, c * LANES:(c + 1) * LANES]

    mix_wait(tok_t, mixed, MIX, 0)
    norm_in(0)
    gather_y(shared, NEAR_Y, 0).start()
    mix_wait(tok_t, mixed, MIX, 1)
    each_block(lambda q: gather_z(shared, GATHER, 0, q).start())
    norm_in(1)
    gather_y(shared, NEAR_Y, 1).start()

    def gather_turn(ref, sem):
        def step(q):
            gather_z(ref, sem, 0, q).wait_recv()
            gather_on(ref, sem, 0, q).start()
            if sem != GATHER:
                gather_z(ref, sem, 1, q).start()

        each_block(step)
        if sem == GATHER:
            each_block(lambda q: gather_z(ref, sem, 1, q).start())

    def gather_end(ref, sem, near, c):
        gather_y(ref, near, c).wait_recv()
        each_block(lambda q: gather_on(ref, sem, c, q).wait_recv())

    def forward_on(ref, sem, q):
        gather_z(ref, sem, 1, q).wait_recv()
        gather_on(ref, sem, 1, q).start()

    def down_block(q):
        w_down(q).wait_recv()
        transpose_down(down_far, 1, q)
        down(0, q)

    def pass_f(c, q):
        pass_on(part_f, near_f, passed_f, far_f, SCATTER, c, q)

    def pass_b(c, q):
        pass_on(part_b, near_b, passed_b, far_b, SCATTER_BACK, c, q)

    gather_turn(shared, GATHER)
    w_up().wait_recv()
    transpose_up(up_far, 1)
    gather_end(shared, GATHER, NEAR_Y, 0)
    up(0)
    for q in range(BLOCKS - 1):
        down_block(q)
        forward_on(shared, GATHER, q)
    pass_f(0, 0)
    down_block(3)
    scatter_own(part_f, near_f, SCATTER_OWN, 0).start()
    forward_on(shared, GATHER, 3)
    shared_on(0).start()
    pass_f(0, 1)
    pass_f(0, 2)
    gather_end(shared, GATHER, NEAR_Y, 1)
    shared_on(1).start()
    pass_f(0, 3)
    up(1)
    each_block(lambda q: down(1, q))
    scatter_own(part_f, near_f, SCATTER_OWN, 1).start()
    each_block(lambda q: pass_f(1, q))
    each_block(lambda q: scatter_z(passed_f, far_f, SCATTER, 0, q).wait_recv())
    scatter_own(part_f, near_f, SCATTER_OWN, 0).wait_recv()
    norm_out(0)
    gather_y(gffn, NEAR_Y_BACK, 0).start()
    each_block(lambda q: gather_z(gffn, GATHER_BACK, 0, q).start())
    each_block(lambda q: scatter_z(passed_f, far_f, SCATTER, 1, q).wait_recv())
    scatter_own(part_f, near_f, SCATTER_OWN, 1).wait_recv()
    norm_out(1)
    gather_y(gffn, NEAR_Y_BACK, 1).start()
    write_out(0)
    gather_turn(gffn, GATHER_BACK)
    write_out(1)
    gather_end(gffn, GATHER_BACK, NEAR_Y_BACK, 0)
    hidden_back(0)
    hidden_on(0).start()

    def back_block(q):
        shared_back(0, q)
        forward_on(gffn, GATHER_BACK, q)

    each_block(back_block)
    scatter_own(part_b, near_b, SCATTER_OWN_BACK, 0).start()
    each_block(lambda q: pass_b(0, q))
    gather_end(gffn, GATHER_BACK, NEAR_Y_BACK, 1)
    hidden_back(1)
    hidden_on(1).start()
    each_block(lambda q: shared_back(1, q))
    scatter_own(part_b, near_b, SCATTER_OWN_BACK, 1).start()
    grad_down(1, gdown_out)
    g_down().start()
    pass_b(1, 0)
    each_block(lambda q: scatter_z(passed_b, far_b, SCATTER_BACK, 0, q).wait_recv())
    scatter_own(part_b, near_b, SCATTER_OWN_BACK, 0).wait_recv()
    sum_back(0)
    mix_start(gsum16, mixed_back, MIX_BACK, 0)
    pl.loop(1, BLOCKS)(lambda q: pass_b(1, q))
    grad_down(0, gdown_ref)
    each_block(lambda q: scatter_z(passed_b, far_b, SCATTER_BACK, 1, q).wait_recv())
    scatter_own(part_b, near_b, SCATTER_OWN_BACK, 1).wait_recv()
    sum_back(1)
    mix_start(gsum16, mixed_back, MIX_BACK, 1)
    for c in range(CHUNKS):
        shared_on(c).wait_recv()
    hidden_on(0).wait_recv()
    grad_up()
    hidden_on(1).wait_recv()
    grad_up_end()
    g_down().wait_recv()
    gdown_ref[...] += gdown_in[...].astype(F32)
    for c in range(CHUNKS):
        mix_wait(gsum16, mixed_back, MIX_BACK, c)
        tokens_back(c)
    for copy in [w_up(), g_down(), shared_on(0), shared_on(1), hidden_on(0), hidden_on(1)]:
        copy.wait_send()
    each_block(lambda q: w_down(q).wait_send())
    for c in range(CHUNKS):
        gather_y(shared, NEAR_Y, c).wait_send()
        gather_y(gffn, NEAR_Y_BACK, c).wait_send()
        scatter_own(part_f, near_f, SCATTER_OWN, c).wait_send()
        scatter_own(part_b, near_b, SCATTER_OWN_BACK, c).wait_send()

        def drain(q):
            gather_z(shared, GATHER, c, q).wait_send()
            gather_on(shared, GATHER, c, q).wait_send()
            scatter_y(part_f, near_f, SCATTER, c, q).wait_send()
            scatter_z(passed_f, far_f, SCATTER, c, q).wait_send()
            gather_z(gffn, GATHER_BACK, c, q).wait_send()
            gather_on(gffn, GATHER_BACK, c, q).wait_send()
            scatter_y(part_b, near_b, SCATTER_BACK, c, q).wait_send()
            scatter_z(passed_b, far_b, SCATTER_BACK, c, q).wait_send()

        each_block(drain)


def on_device(tokens, w_up, w_down, cotangent):
    count, _, width = tokens.shape
    own = w_up.shape[2]
    n_token = lax.axis_size("token")
    head = width // n_token
    samples = CHUNKS * WIDE
    vmem = pl.BlockSpec(memory_space=pltpu.VMEM)

    def blocks(dtype):
        return pltpu.VMEM((CHUNKS, width, LANES), dtype)

    def scatter_scratch():
        return [
            pltpu.VMEM((width, samples), BF16),
            pltpu.VMEM((CHUNKS, width, 2 * LANES), BF16),
            blocks(BF16),
            blocks(BF16),
        ]

    output, grad_tokens, grad_up, grad_down = pl.pallas_call(
        functools.partial(kernel, n_token, head),
        out_shape=(
            pltpu.VMEM((count, width), BF16),
            pltpu.VMEM((count, width), BF16),
            pltpu.VMEM((width, own), F32),
            pltpu.VMEM((own, width), F32),
        ),
        in_specs=[vmem] * 4,
        out_specs=(vmem,) * 4,
        scratch_shapes=[
            blocks(BF16), blocks(BF16), blocks(BF16),
            pltpu.VMEM((width, own), BF16), pltpu.VMEM((own, width), BF16),
            pltpu.VMEM((2 * own, width), BF16), pltpu.VMEM((width, 2 * own), BF16),
            pltpu.VMEM((width, samples), BF16),
            pltpu.VMEM((2 * own, samples), BF16), pltpu.VMEM((2 * own, samples), BF16),
            pltpu.VMEM((width, samples), BF16),
            pltpu.VMEM((2 * own, samples), BF16),
            *scatter_scratch(), *scatter_scratch(),
            blocks(F32), pltpu.VMEM((CHUNKS, 8, LANES), F32), blocks(F32), blocks(F32), blocks(BF16), blocks(BF16),
            pltpu.VMEM((width, samples), BF16), pltpu.VMEM((own, samples), BF16),
            pltpu.VMEM((own, width), BF16), pltpu.VMEM((own, width), BF16),
            pltpu.SemaphoreType.DMA((COPIES,)), pltpu.SemaphoreType.DMA((COPIES,)),
        ],
        compiler_params=pltpu.CompilerParams(
            collective_id=0, has_side_effects=True, vmem_limit_bytes=50 * 1024 * 1024
        ),
        name="rankmixer",
    )(tokens[:, 0], w_up[0], w_down[0], cotangent[:, 0])
    return output[:, None], grad_tokens[:, None], grad_up[None], grad_down[None]


def solution(mesh):
    specs = (
        P("dp", "token", None),
        P("token", None, "dp"),
        P("token", "dp", None),
    )
    in_specs = specs + (specs[0],)
    out_specs = (specs[0], specs[0], specs[1], specs[2])
    return jax.shard_map(
        on_device, mesh=mesh, in_specs=in_specs, out_specs=out_specs, check_vma=False
    )
```

```python
import functools

import jax
import jax.numpy as jnp
from jax import lax
from jax.experimental import pallas as pl
from jax.experimental.pallas import tpu as pltpu
from jax.sharding import PartitionSpec as P

MESH = pl.DeviceIdType.MESH
EPSILON = 1e-05
CHUNKS = 2
LANES = 128
GROUP = 4
WIDE = GROUP * LANES
MXU_ROWS = 256
F32 = jnp.float32
BF16 = jnp.bfloat16

BLOCKS = 4

SPAN = CHUNKS * BLOCKS
MIX, MIX_BACK, UP, GRAD_DOWN, NEAR_Y, NEAR_Y_BACK, SHARED, HIDDEN = 0, 2, 4, 5, 6, 8, 10, 12
SCATTER_OWN, SCATTER_OWN_BACK = 14, 16
DOWN = 18
GATHER = DOWN + BLOCKS
SCATTER = GATHER + 2 * SPAN
GATHER_BACK = SCATTER + 2 * SPAN
SCATTER_BACK = GATHER_BACK + 2 * SPAN
COPIES = SCATTER_BACK + 2 * SPAN


def dot_nn(a, b):
    return jnp.dot(a, b, preferred_element_type=F32)


def dot_nt(a, b):
    return lax.dot_general(a, b, (((1,), (1,)), ((), ())), preferred_element_type=F32)


def layer_norm(values):
    centred = values - jnp.mean(values, axis=0, keepdims=True)
    scaling = lax.rsqrt(jnp.mean(centred * centred, axis=0, keepdims=True) + EPSILON)
    return centred * scaling, scaling


def norm_back(normed, scaling, upstream):
    first = jnp.mean(upstream, axis=0, keepdims=True)
    second = jnp.mean(upstream * normed, axis=0, keepdims=True)
    return scaling * (upstream - first - normed * second)


def gelu_and_slope(v):
    root = 0.7978845608028654
    square = v * v
    t = jnp.tanh(v * (root + (root * 0.044715) * square))
    half = 0.5 * (1.0 + t)
    inner = root + (3.0 * root * 0.044715) * square
    slope = half + (0.5 * v) * (1.0 - t * t) * inner
    return v * half, slope


def kernel(
    n_token, head,
    tok_ref, up_ref, down_ref, cot_ref,
    out_ref, gtok_ref, gup_ref, gdown_ref,
    tok_t, mixed, cot_t, up_far, down_far, up_t, down_t,
    shared, activ, slope, gffn, ghid,
    part_f, near_f, passed_f, far_f, part_b, near_b, passed_b, far_b,
    normed, scale_in, gout, gsum, gsum16, mixed_back,
    shared_far, ghid_far, gdown_out, gdown_in,
    send, recv,
):
    dp = lax.axis_index("dp")
    me = lax.axis_index("token")
    y, zh = dp // 2, dp % 2
    dev_y = ((y + 1 - 2 * (y % 2)) * 2 + zh, me)
    dev_z = (y * 2 + 1 - zh, me)
    dev_w = ((3 - y) * 2 + zh, me)
    d_model, own = up_ref.shape

    def remote(src, dst, sem, device):
        return pltpu.make_async_remote_copy(
            src_ref=src, dst_ref=dst, send_sem=send.at[sem], recv_sem=recv.at[sem],
            device_id=device, device_id_type=MESH,
        )

    block = d_model // BLOCKS

    def rows(i, n):
        return pl.ds(i * n if isinstance(i, int) else pl.multiple_of(i * n, n), n)

    def piece(ref, c, p, n=1, q=None):
        r = slice(None) if q is None else rows(q, block)
        return ref.at[r, pl.ds(c * WIDE + p * LANES, n * LANES)]

    barrier = pltpu.get_barrier_semaphore()

    @pl.loop(1, n_token)
    def _(i):
        pl.semaphore_signal(barrier, inc=1, device_id=(dp, (me + i) % n_token), device_id_type=MESH)

    for device in (dev_y, dev_z, dev_w):
        pl.semaphore_signal(barrier, inc=1, device_id=device, device_id_type=MESH)

    @pl.loop(0, d_model // LANES)
    def _(i):
        block = tok_ref[:, rows(i, LANES)].T
        for c in range(CHUNKS):
            tok_t[c, rows(i, LANES), :] = block[:, c * LANES:(c + 1) * LANES]

    pl.semaphore_wait(barrier, n_token + 2)

    def w_up():
        return remote(up_ref, up_far, UP, dev_w)

    def w_down(q):
        r = rows(q, block)
        return remote(down_ref.at[:, r], down_far.at[:, r], DOWN + q, dev_w)

    def shared_on(c):
        span = pl.ds(c * WIDE, WIDE)
        return remote(shared.at[:, span], shared_far.at[:, span], SHARED + c, dev_w)

    def hidden_on(c):
        span = pl.ds(c * WIDE, WIDE)
        return remote(ghid.at[pl.ds(own, own), span], ghid_far.at[:, span], HIDDEN + c, dev_w)

    def g_down():
        return remote(gdown_out, gdown_in, GRAD_DOWN, dev_w)

    def mix_start(src, dst, sem, c):
        @pl.loop(1, n_token)
        def _(i):
            to = (me + i) % n_token
            remote(
                src.at[c, rows(to, head), :], dst.at[c, rows(me, head), :], sem + c, (dp, to)
            ).start()

        dst[c, rows(me, head), :] = src[c, rows(me, head), :]

    def mix_wait(src, dst, sem, c):
        span = pl.ds(0, (n_token - 1) * head)
        whole = remote(src.at[c, span, :], dst.at[c, span, :], sem + c, dev_y)
        whole.wait_send()
        whole.wait_recv()

    def gather_y(ref, sem, c):
        return remote(piece(ref, c, 0), piece(ref, c, 2), sem + c, dev_y)

    def gather_z(ref, sem, c, q):
        return remote(piece(ref, c, 0, 1, q), piece(ref, c, 1, 1, q), sem + c * BLOCKS + q, dev_z)

    def gather_on(ref, sem, c, q):
        return remote(piece(ref, c, 1, 1, q), piece(ref, c, 3, 1, q), sem + SPAN + c * BLOCKS + q, dev_y)

    def scatter_y(part, near, sem, c, q):
        r = rows(q, block)
        return remote(piece(part, c, 3, 1, q), near.at[c, r, pl.ds(LANES, LANES)], sem + c * BLOCKS + q, dev_y)

    def scatter_own(part, near, sem, c):
        return remote(piece(part, c, 2), near.at[c, :, pl.ds(0, LANES)], sem + c, dev_y)

    def scatter_z(passed, far, sem, c, q):
        r = rows(q, block)
        return remote(passed.at[c, r, :], far.at[c, r, :], sem + SPAN + c * BLOCKS + q, dev_z)

    def each_block(step):
        pl.loop(0, BLOCKS)(step)

    def transpose_up(src, half):
        @pl.loop(0, own // LANES)
        def _(i):
            up_t[pl.ds(pl.multiple_of(half * own + i * LANES, LANES), LANES), :] = src[:, rows(i, LANES)].T

    def transpose_down(src, half, q):
        for i in range(block // LANES):
            r = pl.ds(q * block + i * LANES, LANES)
            down_t[r, pl.ds(half * own, own)] = src[:, r].T

    def norm_in(c):
        summed = mixed[c].astype(F32) + tok_t[c].astype(F32)
        value, scaling = layer_norm(summed)
        normed[c] = value
        scale_in[c, 0:1, :] = scaling
        shared[:, c * WIDE:c * WIDE + LANES] = value.astype(BF16)

    def up(c):
        span = pl.ds(c * WIDE, WIDE)

        @pl.loop(0, 2 * own // MXU_ROWS)
        def _(i):
            r = rows(i, MXU_ROWS)
            hidden = dot_nn(up_t[r, :], shared[:, span])
            value, grade = gelu_and_slope(hidden)
            activ[r, span] = value.astype(BF16)
            slope[r, span] = grade.astype(BF16)

    def down(c, q):
        r = rows(q, block)
        for p in (2, 0):
            span = pl.ds(c * WIDE + p * LANES, 2 * LANES)
            part_f[r, span] = dot_nn(down_t[r, :], activ[:, span]).astype(BF16)
            if p == 2:
                scatter_y(part_f, near_f, SCATTER, c, q).start()

    def pass_on(part, near, passed, far, sem, c, q):
        r = rows(q, block)
        scatter_y(part, near, sem, c, q).wait_recv()
        passed[c, r, :] = (
            part[r, c * WIDE + LANES:c * WIDE + 2 * LANES].astype(F32) + near[c, r, LANES:].astype(F32)
        ).astype(BF16)
        scatter_z(passed, far, sem, c, q).start()

    def total(part, near, far, c):
        return (
            part[:, c * WIDE:c * WIDE + LANES].astype(F32)
            + near[c, :, :LANES].astype(F32)
            + far[c].astype(F32)
        )

    def norm_out(c):
        ffn = total(part_f, near_f, far_f, c)
        value, scaling = layer_norm(ffn + shared[:, c * WIDE:c * WIDE + LANES].astype(F32))
        part_f[:, c * WIDE:c * WIDE + LANES] = value.astype(BF16)
        grad = norm_back(value, scaling, cot_t[c].astype(F32))
        gout[c] = grad
        gffn[:, c * WIDE:c * WIDE + LANES] = grad.astype(BF16)

    def write_out(c):
        @pl.loop(0, d_model // LANES)
        def _(i):
            out_ref[pl.ds(c * LANES, LANES), rows(i, LANES)] = part_f[rows(i, LANES), pl.ds(c * WIDE, LANES)].T

    def hidden_back(c):
        span = pl.ds(c * WIDE, WIDE)
        for half, src in enumerate((down_ref, down_far)):
            @pl.loop(0, own // MXU_ROWS)
            def _(i):
                r = pl.ds(pl.multiple_of(half * own + i * MXU_ROWS, MXU_ROWS), MXU_ROWS)
                grad = dot_nn(src[rows(i, MXU_ROWS), :], gffn[:, span])
                ghid[r, span] = (grad * slope[r, span].astype(F32)).astype(BF16)

    def shared_back(c, q):
        r = rows(q, block)
        for p in (2, 0):
            span = pl.ds(c * WIDE + p * LANES, 2 * LANES)
            part_b[r, span] = (
                dot_nn(up_ref[r, :], ghid[pl.ds(0, own), span])
                + dot_nn(up_far[r, :], ghid[pl.ds(own, own), span])
            ).astype(BF16)
            if p == 2:
                scatter_y(part_b, near_b, SCATTER_BACK, c, q).start()

    def sum_back(c):
        grad = total(part_b, near_b, far_b, c) + gout[c]
        grad = norm_back(normed[c], scale_in[c, 0:1, :], grad)
        gsum[c] = grad
        gsum16[c] = grad.astype(BF16)

    def tokens_back(c):
        @pl.loop(0, d_model // LANES)
        def _(i):
            r = rows(i, LANES)
            value = (gsum[c, r, :] + mixed_back[c, r, :].astype(F32)).astype(BF16)
            gtok_ref[pl.ds(c * LANES, LANES), r] = value.T

    def grad_down(half, dst):
        @pl.loop(0, own // MXU_ROWS)
        def _(i):
            r = pl.ds(pl.multiple_of(half * own + i * MXU_ROWS, MXU_ROWS), MXU_ROWS)
            dst[rows(i, MXU_ROWS), :] = dot_nt(activ[r, :], gffn[...]).astype(dst.dtype)

    def grad_up():
        @pl.loop(0, d_model // MXU_ROWS)
        def _(i):
            r = rows(i, MXU_ROWS)
            gup_ref[r, :] = dot_nt(shared[r, :], ghid[pl.ds(0, own), :]) + dot_nt(
                shared_far[r, pl.ds(0, WIDE)], ghid_far[:, pl.ds(0, WIDE)]
            )

    def grad_up_end():
        @pl.loop(0, d_model // MXU_ROWS)
        def _(i):
            r = rows(i, MXU_ROWS)
            gup_ref[r, :] += dot_nt(shared_far[r, pl.ds(WIDE, WIDE)], ghid_far[:, pl.ds(WIDE, WIDE)])

    w_up().start()
    for q in range(BLOCKS):
        w_down(q).start()
    for c in range(CHUNKS):
        mix_start(tok_t, mixed, MIX, c)
    transpose_up(up_ref, 0)
    for q in range(BLOCKS):
        transpose_down(down_ref, 0, q)

    @pl.loop(0, d_model // LANES)
    def _(i):
        tile = cot_ref[:, rows(i, LANES)].T
        for c in range(CHUNKS):
            cot_t[c, rows(i, LANES), :] = tile[:, c * LANES:(c + 1) * LANES]

    mix_wait(tok_t, mixed, MIX, 0)
    norm_in(0)
    gather_y(shared, NEAR_Y, 0).start()
    mix_wait(tok_t, mixed, MIX, 1)
    each_block(lambda q: gather_z(shared, GATHER, 0, q).start())
    norm_in(1)
    gather_y(shared, NEAR_Y, 1).start()

    def gather_turn(ref, sem):
        def step(q):
            gather_z(ref, sem, 0, q).wait_recv()
            gather_on(ref, sem, 0, q).start()
            if sem != GATHER:
                gather_z(ref, sem, 1, q).start()

        each_block(step)
        if sem == GATHER:
            each_block(lambda q: gather_z(ref, sem, 1, q).start())

    def gather_end(ref, sem, near, c):
        gather_y(ref, near, c).wait_recv()
        each_block(lambda q: gather_on(ref, sem, c, q).wait_recv())

    def forward_on(ref, sem, q):
        gather_z(ref, sem, 1, q).wait_recv()
        gather_on(ref, sem, 1, q).start()

    def down_block(q):
        w_down(q).wait_recv()
        transpose_down(down_far, 1, q)
        down(0, q)

    def pass_f(c, q):
        pass_on(part_f, near_f, passed_f, far_f, SCATTER, c, q)

    def pass_b(c, q):
        pass_on(part_b, near_b, passed_b, far_b, SCATTER_BACK, c, q)

    gather_turn(shared, GATHER)
    w_up().wait_recv()
    transpose_up(up_far, 1)
    gather_end(shared, GATHER, NEAR_Y, 0)
    up(0)
    for q in range(BLOCKS - 1):
        down_block(q)
        forward_on(shared, GATHER, q)
    pass_f(0, 0)
    down_block(3)
    scatter_own(part_f, near_f, SCATTER_OWN, 0).start()
    forward_on(shared, GATHER, 3)
    shared_on(0).start()
    pass_f(0, 1)
    pass_f(0, 2)
    gather_end(shared, GATHER, NEAR_Y, 1)
    shared_on(1).start()
    pass_f(0, 3)
    up(1)
    each_block(lambda q: down(1, q))
    scatter_own(part_f, near_f, SCATTER_OWN, 1).start()
    each_block(lambda q: pass_f(1, q))
    each_block(lambda q: scatter_z(passed_f, far_f, SCATTER, 0, q).wait_recv())
    scatter_own(part_f, near_f, SCATTER_OWN, 0).wait_recv()
    norm_out(0)
    gather_y(gffn, NEAR_Y_BACK, 0).start()
    each_block(lambda q: gather_z(gffn, GATHER_BACK, 0, q).start())
    each_block(lambda q: scatter_z(passed_f, far_f, SCATTER, 1, q).wait_recv())
    scatter_own(part_f, near_f, SCATTER_OWN, 1).wait_recv()
    norm_out(1)
    gather_y(gffn, NEAR_Y_BACK, 1).start()
    write_out(0)
    gather_turn(gffn, GATHER_BACK)
    write_out(1)
    gather_end(gffn, GATHER_BACK, NEAR_Y_BACK, 0)
    hidden_back(0)
    hidden_on(0).start()

    def back_block(q):
        shared_back(0, q)
        forward_on(gffn, GATHER_BACK, q)

    each_block(back_block)
    scatter_own(part_b, near_b, SCATTER_OWN_BACK, 0).start()
    each_block(lambda q: pass_b(0, q))
    gather_end(gffn, GATHER_BACK, NEAR_Y_BACK, 1)
    hidden_back(1)
    hidden_on(1).start()
    each_block(lambda q: shared_back(1, q))
    scatter_own(part_b, near_b, SCATTER_OWN_BACK, 1).start()
    grad_down(1, gdown_out)
    g_down().start()
    each_block(lambda q: pass_b(1, q))
    each_block(lambda q: scatter_z(passed_b, far_b, SCATTER_BACK, 0, q).wait_recv())
    scatter_own(part_b, near_b, SCATTER_OWN_BACK, 0).wait_recv()
    sum_back(0)
    mix_start(gsum16, mixed_back, MIX_BACK, 0)
    grad_down(0, gdown_ref)
    each_block(lambda q: scatter_z(passed_b, far_b, SCATTER_BACK, 1, q).wait_recv())
    scatter_own(part_b, near_b, SCATTER_OWN_BACK, 1).wait_recv()
    sum_back(1)
    mix_start(gsum16, mixed_back, MIX_BACK, 1)
    for c in range(CHUNKS):
        shared_on(c).wait_recv()
    hidden_on(0).wait_recv()
    grad_up()
    hidden_on(1).wait_recv()
    grad_up_end()
    for c in range(CHUNKS):
        mix_wait(gsum16, mixed_back, MIX_BACK, c)
        tokens_back(c)
    g_down().wait_recv()
    gdown_ref[...] += gdown_in[...].astype(F32)
    for copy in [w_up(), g_down(), shared_on(0), shared_on(1), hidden_on(0), hidden_on(1)]:
        copy.wait_send()
    each_block(lambda q: w_down(q).wait_send())
    for c in range(CHUNKS):
        gather_y(shared, NEAR_Y, c).wait_send()
        gather_y(gffn, NEAR_Y_BACK, c).wait_send()
        scatter_own(part_f, near_f, SCATTER_OWN, c).wait_send()
        scatter_own(part_b, near_b, SCATTER_OWN_BACK, c).wait_send()

        def drain(q):
            gather_z(shared, GATHER, c, q).wait_send()
            gather_on(shared, GATHER, c, q).wait_send()
            scatter_y(part_f, near_f, SCATTER, c, q).wait_send()
            scatter_z(passed_f, far_f, SCATTER, c, q).wait_send()
            gather_z(gffn, GATHER_BACK, c, q).wait_send()
            gather_on(gffn, GATHER_BACK, c, q).wait_send()
            scatter_y(part_b, near_b, SCATTER_BACK, c, q).wait_send()
            scatter_z(passed_b, far_b, SCATTER_BACK, c, q).wait_send()

        each_block(drain)


def on_device(tokens, w_up, w_down, cotangent):
    count, _, width = tokens.shape
    own = w_up.shape[2]
    n_token = lax.axis_size("token")
    head = width // n_token
    samples = CHUNKS * WIDE
    vmem = pl.BlockSpec(memory_space=pltpu.VMEM)

    def blocks(dtype):
        return pltpu.VMEM((CHUNKS, width, LANES), dtype)

    def scatter_scratch():
        return [
            pltpu.VMEM((width, samples), BF16),
            pltpu.VMEM((CHUNKS, width, 2 * LANES), BF16),
            blocks(BF16),
            blocks(BF16),
        ]

    output, grad_tokens, grad_up, grad_down = pl.pallas_call(
        functools.partial(kernel, n_token, head),
        out_shape=(
            pltpu.VMEM((count, width), BF16),
            pltpu.VMEM((count, width), BF16),
            pltpu.VMEM((width, own), F32),
            pltpu.VMEM((own, width), F32),
        ),
        in_specs=[vmem] * 4,
        out_specs=(vmem,) * 4,
        scratch_shapes=[
            blocks(BF16), blocks(BF16), blocks(BF16),
            pltpu.VMEM((width, own), BF16), pltpu.VMEM((own, width), BF16),
            pltpu.VMEM((2 * own, width), BF16), pltpu.VMEM((width, 2 * own), BF16),
            pltpu.VMEM((width, samples), BF16),
            pltpu.VMEM((2 * own, samples), BF16), pltpu.VMEM((2 * own, samples), BF16),
            pltpu.VMEM((width, samples), BF16),
            pltpu.VMEM((2 * own, samples), BF16),
            *scatter_scratch(), *scatter_scratch(),
            blocks(F32), pltpu.VMEM((CHUNKS, 8, LANES), F32), blocks(F32), blocks(F32), blocks(BF16), blocks(BF16),
            pltpu.VMEM((width, samples), BF16), pltpu.VMEM((own, samples), BF16),
            pltpu.VMEM((own, width), BF16), pltpu.VMEM((own, width), BF16),
            pltpu.SemaphoreType.DMA((COPIES,)), pltpu.SemaphoreType.DMA((COPIES,)),
        ],
        compiler_params=pltpu.CompilerParams(
            collective_id=0, has_side_effects=True, vmem_limit_bytes=50 * 1024 * 1024
        ),
        name="rankmixer",
    )(tokens[:, 0], w_up[0], w_down[0], cotangent[:, 0])
    return output[:, None], grad_tokens[:, None], grad_up[None], grad_down[None]


def solution(mesh):
    specs = (
        P("dp", "token", None),
        P("token", None, "dp"),
        P("token", "dp", None),
    )
    in_specs = specs + (specs[0],)
    out_specs = (specs[0], specs[0], specs[1], specs[2])
    return jax.shard_map(
        on_device, mesh=mesh, in_specs=in_specs, out_specs=out_specs, check_vma=False
    )
```
